128 devices in a mesh: row: 16 (over y, x), col: 8 (over z, core).
Axes of the slice: x: 4, y: 4, z: 4, core: 2. Of those that a mesh axis runs over, the one named last changes fastest.
Arguments:
- panel: float32 [64, 65536], P(None, ('row', 'col')), may hold values from -6 to 6
- blocks: bfloat16 [256, 8, 8, 256, 256], P('row', 'col'), may hold values from -100 to 100
- columns: int32 [256, 8, 8], P('row', 'col'), may hold values from 0 to 31
- counts: int32 [256, 8], P('row', 'col'), may hold values from 1 to 8, as said below
Outputs:
- basis: float32 [64, 65536], P(None, ('row', 'col'))
The draws below stay inside these ranges and needn't reach their ends.
Inputs may be any that keep to these rules, and one draw needn't show every extreme that they name: `counts`: every block row has between 1 and 8 live slots in each column group, and both ends occur.
All inputs are finite; a program needn't handle non-finite values.
Results may differ from the reference program's by a relative error of at most 0.008.
Values may be sent and summed in bfloat16 or wider, within the bound.
A program may use at most 64 MiB of HBM per device.

```python
import math
import jax
import jax.numpy as jnp
from jax import lax

BS = 256
P_SIZE = 64
KC = 8
STEPS = 2
NB = 256
BPD = 2
NROWS = 65536
N_ROW = 16
N_COL = 8


LOG_TEN = math.log(10.0)


def draw_counts(key, part):
    key = jax.random.fold_in(key, 7)
    drawn = jax.random.randint(key, (NB, N_COL), 1, KC + 1, dtype=jnp.int32)
    drawn = drawn.at[0, 0].set(KC)
    drawn = drawn.at[1, 0].set(1)
    return drawn


def draw_blocks(key, part):
    key = jax.random.fold_in(key, 11)
    key_values = jax.random.fold_in(key, 1)
    key_rows = jax.random.fold_in(key, 2)
    key_cols = jax.random.fold_in(key, 3)
    uniform_part = jax.random.uniform(key_values, (NB, N_COL, KC, BS, BS), jnp.float32)
    centred = 2.0 * uniform_part - 1.0
    magnitude = 0.25 + 0.75 * jnp.abs(centred)
    signed = jnp.where(centred >= 0.0, magnitude, -magnitude)
    row_factor = jnp.exp(LOG_TEN * jax.random.uniform(key_rows, (NB, 1, 1, BS, 1), jnp.float32))
    col_factor = jnp.exp(LOG_TEN * jax.random.uniform(key_cols, (NB, N_COL, KC, 1, BS), jnp.float32))
    return (signed * row_factor * col_factor).astype(jnp.bfloat16)


def set_ends(entries, stream_key, smallest, top_value):
    index_at = [jax.random.randint(jax.random.fold_in(stream_key, axis), (), 0, length) for axis, length in enumerate(entries.shape)]
    longest = entries.shape.index(max(entries.shape))
    neighbour = index_at[:longest] + [(index_at[longest] + 1) % entries.shape[longest]] + index_at[longest + 1:]
    return entries.at[tuple(index_at)].set(smallest).at[tuple(neighbour)].set(top_value)


def block_scale(stream_key, dims, shards, smallest, high):
    factor_of = 1.0
    for dim, blocks in shards:
        steps = jax.random.uniform(jax.random.fold_in(jax.random.fold_in(stream_key, 6), dim), (blocks,), jnp.float32, smallest / len(shards), high / len(shards))
        factor_of = factor_of * jnp.repeat(jnp.exp(steps), dims[dim] // blocks).reshape((-1,) + (1,) * (len(dims) - 1 - dim))
    return factor_of


def bell_draw(rng, dims, scale, reach, split=(), kind=jnp.bfloat16):
    values = scale * jax.random.normal(rng, dims, jnp.float32)
    if split:
        values = values * block_scale(rng, dims, split, -0.22, 0.18)
    return jnp.clip(values, -reach, reach).astype(kind)


def setup_inputs(seed: int = 0) -> dict:
    key_of = jax.random.split(jax.random.key(seed), 5)
    return {
        "panel": bell_draw(key_of[0], (P_SIZE, NROWS), 1.0, 6.0, ((1, 128),), jnp.float32),
        "blocks": draw_blocks(jax.random.fold_in(key_of[4], 71), 0),
        "columns": set_ends(jax.random.randint(key_of[2], (NB, N_COL, KC), 0, N_ROW * BPD), jax.random.fold_in(key_of[2], 1), 0, (N_ROW * BPD) - 1).astype(jnp.int32),
        "counts": draw_counts(jax.random.fold_in(key_of[4], 71), 0),
    }


def live_slots(counts):
    return (jnp.arange(KC, dtype=jnp.int32)[None, None, :] < counts[:, :, None]).astype(jnp.float32)

def block_targets(columns):
    group = jnp.arange(N_COL, dtype=jnp.int32)[None, :, None]
    return (columns // BPD * N_COL + group) * BPD + columns % BPD

def reference(panel, blocks, columns, counts):
    live = live_slots(counts)
    targets = block_targets(columns).astype(jnp.int32)

    def row_degree(item):
        block_set, alive = item
        return jnp.einsum('jkrs,jk->r', jnp.abs(block_set.astype(jnp.float32)), alive)
    degree = lax.map(row_degree, (blocks, live)).reshape(-1)
    scale = 1.0 / jnp.sqrt(degree)
    state = panel
    for step in range(STEPS):
        sent = (scale[None, :] * state).astype(jnp.bfloat16)
        grid = sent.reshape(P_SIZE, NB, BS)

        def row_product(item):
            block_set, target, alive = item
            picked = grid[:, target.reshape(-1), :].astype(jnp.float32).reshape(P_SIZE, N_COL, KC, BS)
            picked = picked * alive[None, :, :, None]
            return jnp.einsum('pjks,jkrs->pr', picked, block_set.astype(jnp.float32))
        prod = lax.map(row_product, (blocks, targets, live))
        prod = jnp.transpose(prod, (1, 0, 2)).reshape(P_SIZE, NROWS)
        grown = scale[None, :] * prod
        gram = jnp.dot(grown, grown.T, precision=lax.Precision.HIGHEST) / NROWS
        lower = jnp.linalg.cholesky(gram)
        state = lax.linalg.triangular_solve(lower, grown, left_side=True, lower=True)
    return state
```

```python
import functools

import jax
import jax.numpy as jnp
from jax import lax
from jax.experimental import pallas as pl
from jax.experimental.pallas import tpu as pltpu
from jax.sharding import PartitionSpec as P

MESH = pl.DeviceIdType.MESH
HIGHEST = lax.Precision.HIGHEST
F32 = jnp.float32
BF16 = jnp.bfloat16
NT = (((1,), (1,)), ((), ()))
TN = (((0,), (0,)), ((), ()))
SIDE = 4
PANEL = 16

COL_ORDER = ((2, 0), (2, 1), (1, 0), (1, 1), (3, 0), (3, 1), (0, 1))
NEAR_FAR = (1, 3, 2)


def inverse_factor(gram):
    size = gram.shape[0]
    rows = lax.broadcasted_iota(jnp.int32, (size, size), 0)
    lanes = lax.broadcasted_iota(jnp.int32, (size, size), 1)
    whole = jnp.concatenate([gram, (rows == lanes).astype(F32)], axis=1)
    parts = [whole[t * PANEL : (t + 1) * PANEL] for t in range(size // PANEL)]
    below = lax.broadcasted_iota(jnp.int32, (PANEL, 2 * size), 0)
    done = []
    for t in range(len(parts)):
        part = parts[t]
        first = t * PANEL
        column = [jnp.broadcast_to(part[:, first + q : first + q + 1], part.shape) for q in range(PANEL)]
        pivot = jnp.zeros_like(part)
        for q in range(PANEL):
            pivot_row = column[q][q : q + 1]
            pivot = jnp.where(below == q, pivot_row, pivot)
            factor = jnp.where(below > q, column[q] / pivot_row, 0.0)
            part = part - factor * part[q : q + 1]
            for later in range(q + 1, PANEL):
                column[later] = column[later] - factor * column[later][q : q + 1]
        scaled = part / pivot
        for u in range(t + 1, len(parts)):
            parts[u] = parts[u] - lax.dot_general(
                scaled[:, u * PANEL : (u + 1) * PANEL], part, TN, precision=HIGHEST, preferred_element_type=F32
            )
        done.append(part[:, size:] * lax.rsqrt(pivot[:, size:]))
    return jnp.concatenate(done, axis=0)


def pack(gram):
    half = gram.shape[0] // 2
    return jnp.concatenate([gram[:half], gram[half:]], axis=1)


def unpack(packed):
    width = packed.shape[1] // 2
    return jnp.concatenate([packed[:, :width], packed[:, width:]], axis=0)


def kernel(
    panel, blocks, columns, counts, gram_out, grown_out,
    stored, first, second, scales, own_scale, deg_out, deg_in, part_out, part_in, part_own,
    gram_a_out, gram_a_in, gram_b_out, gram_b_in, grown,
    load_sem, deg_s, deg_r, scale_s, scale_r, gather_s, gather_r, part_s, part_r, ga_s, ga_r, gb_s, gb_r,
):
    row, col = lax.axis_index("row"), lax.axis_index("col")
    y, x = row // SIDE, row % SIDE
    z, core = col // 2, col % 2
    block_rows, slots = columns.shape[0], columns.shape[2]
    sites = 65536

    def chip(dy, dx):
        return ((y + dy) % SIDE) * SIDE + (x + dx) % SIDE

    def column_of(dz, dc):
        return ((z + dz) % SIDE) * 2 + (core + dc) % 2

    def source_of(dz, dc):
        return ((z + SIDE - dz) % SIDE) * 2 + (core + dc) % 2

    def send(src, dst, send_sem, recv_sem, to):
        return pltpu.make_async_remote_copy(
            src_ref=src, dst_ref=dst, send_sem=send_sem, recv_sem=recv_sem, device_id=to, device_id_type=MESH
        )

    loads = [
        pltpu.make_async_copy(blocks.at[i, 0], stored.at[pl.ds(i * slots, slots)], load_sem.at[i])
        for i in range(block_rows)
    ]
    for load in loads:
        load.start()

    barrier = pltpu.get_barrier_semaphore()
    row_offsets = [(dy, dx) for dy in (0, 1, 3, 2) for dx in (0, 1, 3, 2) if (dy, dx) != (0, 0)]
    for dy, dx in row_offsets:
        pl.semaphore_signal(barrier, inc=1, device_id=(chip(dy, dx), col), device_id_type=MESH)
    for dz, dc in COL_ORDER:
        pl.semaphore_signal(barrier, inc=1, device_id=(row, column_of(dz, dc)), device_id_type=MESH)

    mine = pl.ds(row * 2, 2)
    for half in range(2):
        first[row * 2 + half] = panel[:, half * 256 : (half + 1) * 256].astype(BF16)
    first[32] = jnp.zeros_like(first[32])
    second[32] = jnp.zeros_like(second[32])
    pl.semaphore_wait(barrier, len(row_offsets) + len(COL_ORDER))

    def forward(buf, turn, half, src, to, k):
        (sy, sx), (ty, tx) = src, to
        piece = chip(SIDE - sy, SIDE - sx) * 2 + half
        arrives = half * 16 + ((sy + ty) % SIDE) * SIDE + (sx + tx) % SIDE
        return send(buf.at[piece], buf.at[piece], gather_s.at[turn, k], gather_r.at[turn, arrives], (chip(ty, tx), col))

    def gather_start(buf, turn):
        copies = []
        for d in NEAR_FAR:
            copies.append(forward(buf, turn, 0, (0, 0), (0, d), len(copies)))
            copies[-1].start()
            copies.append(forward(buf, turn, 1, (0, 0), (d, 0), len(copies)))
            copies[-1].start()
        for d in NEAR_FAR:
            copies.append(forward(buf, turn, 0, (0, 0), (d, 0), len(copies)))
            copies[-1].start()
            copies.append(forward(buf, turn, 1, (0, 0), (0, d), len(copies)))
            copies[-1].start()
        return copies

    def arrived(buf, turn, half, dy, dx):
        piece = chip(SIDE - dy, SIDE - dx) * 2 + half
        send(
            buf.at[piece], buf.at[piece], gather_s.at[turn, 0], gather_r.at[turn, half * 16 + dy * SIDE + dx], (row, col)
        ).wait_recv()

    def gather_forward(buf, turn, copies):
        for d in NEAR_FAR:
            arrived(buf, turn, 0, 0, d)
            for e in NEAR_FAR:
                copies.append(forward(buf, turn, 0, (0, d), (e, 0), len(copies)))
                copies[-1].start()
            arrived(buf, turn, 1, d, 0)
            for e in NEAR_FAR:
                copies.append(forward(buf, turn, 1, (d, 0), (0, e), len(copies)))
                copies[-1].start()

    def gather_end(buf, turn, copies):
        for e in NEAR_FAR:
            for d in range(SIDE):
                arrived(buf, turn, 0, e, d)
                arrived(buf, turn, 1, d, e)
        for copy in copies:
            copy.wait_send()

    copies = gather_start(first, 0)

    for i in range(block_rows):
        loads[i].wait()
        total = jnp.zeros((8, 256), F32)
        for s in range(slots):
            alive = jnp.where(s < counts[i, 0], 1.0, 0.0).astype(F32)
            ones = jnp.full((8, 256), alive, F32).astype(BF16)
            total += lax.dot_general(ones, jnp.abs(stored[i * slots + s]), NT, preferred_element_type=F32)
        deg_out[i // 2, i % 2] = total[:1]
        if i == 11:
            gather_forward(first, 0, copies)

    deg_copies = []
    for k, (dz, dc) in enumerate(COL_ORDER):
        to = column_of(dz, dc)
        deg_copies.append(send(deg_out.at[to], deg_in.at[k], deg_s.at[k], deg_r.at[k], (row, to)))
        deg_copies[-1].start()
    degree = deg_out[col]
    for k, copy in enumerate(deg_copies):
        copy.wait_recv()
        degree = degree + deg_in[k]
    own_scale[...] = 1.0 / jnp.sqrt(degree)
    scales[mine] = own_scale[...]
    scale_copies = []
    for k, (dy, dx) in enumerate(row_offsets):
        scale_copies.append(
            send(own_scale, scales.at[mine], scale_s.at[k], scale_r.at[k], (chip(dy, dx), col))
        )
        scale_copies[-1].start()
    gather_end(first, 0, copies)
    for k, (dy, dx) in enumerate(row_offsets):
        theirs = pl.ds(chip(SIDE - dy, SIDE - dx) * 2, 2)
        send(own_scale, scales.at[theirs], scale_s.at[k], scale_r.at[k], (row, col)).wait_recv()

    def scale_block(g, carry):
        first[g] = (first[g].astype(F32) * scales[g]).astype(BF16)
        return carry

    lax.fori_loop(0, 32, scale_block, 0, unroll=4)

    def product(buf, turn):
        started = []
        for k, (dz, dc) in enumerate(COL_ORDER + ((0, 0),)):
            to = column_of(dz, dc)
            for half in range(2):
                i = to * 2 + half
                total = jnp.zeros((64, 256), F32)
                for s in range(slots):
                    g = jnp.where(s < counts[i, 0], columns[i, 0, s], 32)
                    total += lax.dot_general(buf[g], stored[i * slots + s], NT, preferred_element_type=F32)
                if k < len(COL_ORDER):
                    part_out[turn, k, half] = total.astype(BF16)
                else:
                    part_own[half] = total
            if k < len(COL_ORDER):
                started.append(
                    send(part_out.at[turn, k], part_in.at[turn, k], part_s.at[turn, k], part_r.at[turn, k], (row, to))
                )
                started[-1].start()
        return started

    def summed(started, turn):
        total = part_own[...]
        for k, copy in enumerate(started):
            copy.wait_recv()
            total = total + part_in[turn, k].astype(F32)
        for copy in started:
            copy.wait_send()
        return total

    def local_gram(values):
        return sum(
            lax.dot_general(values[h], values[h], NT, precision=HIGHEST, preferred_element_type=F32) for h in range(2)
        )

    def gram_col_start(gram, turn):
        gram_a_out[turn] = pack(gram)
        started = []
        for k, (dz, dc) in enumerate(COL_ORDER):
            started.append(
                send(
                    gram_a_out.at[turn], gram_a_in.at[turn, k], ga_s.at[turn, k], ga_r.at[turn, k],
                    (row, column_of(dz, dc)),
                )
            )
            started[-1].start()
        return started

    def gram_row_start(started, turn):
        total = gram_a_out[turn]
        for k, copy in enumerate(started):
            copy.wait_recv()
            total = total + gram_a_in[turn, k]
        gram_b_out[turn] = total
        onward = []
        for k, (dy, dx) in enumerate(row_offsets):
            onward.append(
                send(gram_b_out.at[turn], gram_b_in.at[turn, k], gb_s.at[turn, k], gb_r.at[turn, k], (chip(dy, dx), col))
            )
            onward[-1].start()
        for copy in started:
            copy.wait_send()
        return onward

    def gram_end(onward, turn):
        total = gram_b_out[turn]
        for k, copy in enumerate(onward):
            copy.wait_recv()
            total = total + gram_b_in[turn, k]
        for copy in onward:
            copy.wait_send()
        return unpack(total) / sites

    started = product(first, 0)
    for copy in deg_copies + scale_copies:
        copy.wait_send()
    grown[...] = summed(started, 0) * own_scale[...]
    second[mine] = (grown[...] * own_scale[...]).astype(BF16)
    copies = gather_start(second, 1)
    gram_copies = gram_col_start(local_gram(grown), 0)
    gather_forward(second, 1, copies)
    gram_copies = gram_row_start(gram_copies, 0)
    gather_end(second, 1, copies)

    started = product(second, 1)
    inverse = inverse_factor(gram_end(gram_copies, 0))
    raw = summed(started, 1) * own_scale[...]
    for half in range(2):
        grown[half] = jnp.dot(inverse, raw[half], precision=HIGHEST, preferred_element_type=F32)
    grown_out[...] = grown[...]
    gram_copies = gram_col_start(local_gram(grown), 1)
    gram_copies = gram_row_start(gram_copies, 1)
    gram_out[...] = gram_end(gram_copies, 1)


def finish(gram, grown, out):
    inverse = inverse_factor(gram[...])
    for half in range(2):
        out[:, half * 256 : (half + 1) * 256] = jnp.dot(
            inverse, grown[half], precision=HIGHEST, preferred_element_type=F32
        )


def per_device(panel, blocks, columns, counts):
    vmem = pl.BlockSpec(memory_space=pltpu.VMEM)
    smem = pl.BlockSpec(memory_space=pltpu.SMEM)
    dma = pltpu.SemaphoreType.DMA
    gram, grown = pl.pallas_call(
        kernel,
        out_shape=(jax.ShapeDtypeStruct((64, 64), F32), jax.ShapeDtypeStruct((2, 64, 256), F32)),
        in_specs=[vmem, pl.BlockSpec(memory_space=pl.ANY), smem, smem],
        out_specs=(vmem, vmem),
        scratch_shapes=[
            pltpu.VMEM((128, 256, 256), BF16),
            pltpu.VMEM((33, 64, 256), BF16),
            pltpu.VMEM((33, 64, 256), BF16),
            pltpu.VMEM((32, 1, 256), F32),
            pltpu.VMEM((2, 1, 256), F32),
            pltpu.VMEM((8, 2, 1, 256), F32),
            pltpu.VMEM((7, 2, 1, 256), F32),
            pltpu.VMEM((2, 7, 2, 64, 256), BF16),
            pltpu.VMEM((2, 7, 2, 64, 256), BF16),
            pltpu.VMEM((2, 64, 256), F32),
            pltpu.VMEM((2, 32, 128), F32),
            pltpu.VMEM((2, 7, 32, 128), F32),
            pltpu.VMEM((2, 32, 128), F32),
            pltpu.VMEM((2, 15, 32, 128), F32),
            pltpu.VMEM((2, 64, 256), F32),
            dma((16,)),
            dma((7,)),
            dma((7,)),
            dma((15,)),
            dma((15,)),
            dma((2, 30)),
            dma((2, 32)),
            dma((2, 7)),
            dma((2, 7)),
            dma((2, 7)),
            dma((2, 7)),
            dma((2, 15)),
            dma((2, 15)),
        ],
        compiler_params=pltpu.CompilerParams(
            collective_id=0, has_side_effects=True, vmem_limit_bytes=48 * 2**20
        ),
    )(panel, blocks, columns, counts)
    return pl.pallas_call(
        finish,
        out_shape=jax.ShapeDtypeStruct(panel.shape, F32),
        in_specs=[vmem, vmem],
        out_specs=vmem,
    )(gram, grown)


def solution(mesh):
    in_specs = (
        P(None, ("row", "col")),
        P("row", "col", None, None, None),
        P("row", "col", None),
        P("row", "col"),
    )
    return jax.shard_map(
        per_device, mesh=mesh, in_specs=in_specs, out_specs=P(None, ("row", "col")), check_vma=False
    )
```

```python
import functools

import jax
import jax.numpy as jnp
from jax import lax
from jax.experimental import pallas as pl
from jax.experimental.pallas import tpu as pltpu
from jax.sharding import PartitionSpec as P

MESH = pl.DeviceIdType.MESH
HIGHEST = lax.Precision.HIGHEST
F32 = jnp.float32
BF16 = jnp.bfloat16
NT = (((1,), (1,)), ((), ()))
SIDE = 4
PANEL = 16

COL_ORDER = ((2, 0), (2, 1), (1, 0), (1, 1), (3, 0), (3, 1), (0, 1))
NEAR_FAR = (1, 3, 2)


def inverse_factor(gram):
    size = gram.shape[0]
    rows = lax.broadcasted_iota(jnp.int32, (size, size), 0)
    lanes = lax.broadcasted_iota(jnp.int32, (size, size), 1)
    rest = jnp.concatenate([gram, (rows == lanes).astype(F32)], axis=1)
    done = []
    for first in range(0, size, PANEL):
        below = lax.broadcasted_iota(jnp.int32, rest.shape, 0)
        column = [jnp.broadcast_to(rest[:, first + q : first + q + 1], rest.shape) for q in range(PANEL)]
        pivots = []
        for q in range(PANEL):
            pivot = column[q][q : q + 1]
            pivots.append(pivot)
            factor = jnp.where(below > q, column[q] * (1.0 / pivot), 0.0)
            rest = rest - factor * rest[q : q + 1]
            for later in range(q + 1, PANEL):
                column[later] = column[later] - factor * column[later][q : q + 1]
        done.append(rest[:PANEL, size:] * lax.rsqrt(jnp.concatenate(pivots, axis=0)[:, size:]))
        rest = rest[PANEL:]
    return jnp.concatenate(done, axis=0)


def pack(gram):
    half = gram.shape[0] // 2
    return jnp.concatenate([gram[:half], gram[half:]], axis=1)


def unpack(packed):
    width = packed.shape[1] // 2
    return jnp.concatenate([packed[:, :width], packed[:, width:]], axis=0)


def kernel(
    panel, blocks, columns_hbm, counts_hbm, out,
    stored, start, columns, counts, first, second, scales, own_scale, deg_out, deg_in, part_out, part_in, part_own,
    piece_out, piece_in, piece_sum, piece_row, piece_all, gram_out, gram_in, cross_out, cross_in, grown,
    small_sem, load_sem, deg_s, deg_r, scale_s, scale_r, gather_s, gather_r, part_s, part_r,
    pa_s, pa_r, pb_s, pb_r, pc_s, pc_r, ga_s, ga_r, gb_s, gb_r,
):
    row, col = lax.axis_index("row"), lax.axis_index("col")
    y, x = row // SIDE, row % SIDE
    z, core = col // 2, col % 2
    slots, block_rows = columns.shape
    sites = 65536

    def chip(dy, dx):
        return ((y + dy) % SIDE) * SIDE + (x + dx) % SIDE

    def column_of(dz, dc):
        return ((z + dz) % SIDE) * 2 + (core + dc) % 2

    def send(src, dst, send_sem, recv_sem, to):
        return pltpu.make_async_remote_copy(
            src_ref=src, dst_ref=dst, send_sem=send_sem, recv_sem=recv_sem, device_id=to, device_id_type=MESH
        )

    small = [
        pltpu.make_async_copy(panel, start, small_sem.at[0]),
        pltpu.make_async_copy(counts_hbm, counts, small_sem.at[1]),
        pltpu.make_async_copy(columns_hbm.at[0], columns, small_sem.at[2]),
    ]
    loads = [
        pltpu.make_async_copy(blocks.at[i, 0], stored.at[pl.ds(i * slots, slots)], load_sem.at[i])
        for i in range(block_rows)
    ]
    for load in small + loads:
        load.start()

    barrier = pltpu.get_barrier_semaphore()
    row_offsets = [(dy, dx) for dy in (2, 1, 3, 0) for dx in (2, 1, 3, 0) if (dy, dx) != (0, 0)]
    for dy, dx in row_offsets:
        pl.semaphore_signal(barrier, inc=1, device_id=(chip(dy, dx), col), device_id_type=MESH)
    for dz, dc in COL_ORDER:
        pl.semaphore_signal(barrier, inc=1, device_id=(row, column_of(dz, dc)), device_id_type=MESH)

    mine = pl.ds(row * 2, 2)
    first[32] = jnp.zeros_like(first[32])
    second[32] = jnp.zeros_like(second[32])
    for load in small:
        load.wait()
    for half in range(2):
        first[row * 2 + half] = start[:, half * 256 : (half + 1) * 256].astype(BF16)

    def forward(buf, turn, half, src, to, copies):
        (sy, sx), (ty, tx) = src, to
        piece = chip(SIDE - sy, SIDE - sx) * 2 + half
        arrives = ((sy + ty) % SIDE) * SIDE + (sx + tx) % SIDE
        copies.append(
            send(
                buf.at[piece], buf.at[piece], gather_s.at[turn, half, len(copies)], gather_r.at[turn, half, arrives],
                (chip(ty, tx), col),
            )
        )
        copies[-1].start()

    def turned(half, one, other):
        return (other, one) if half == 0 else (one, other)

    def gather_start(buf, turn, half):
        copies = []
        for d in NEAR_FAR:
            forward(buf, turn, half, (0, 0), turned(half, d, 0), copies)
        for d in NEAR_FAR:
            forward(buf, turn, half, (0, 0), turned(half, 0, d), copies)
        return copies

    def arrived(buf, turn, half, offset):
        dy, dx = offset
        piece = buf.at[chip(SIDE - dy, SIDE - dx) * 2 + half]
        send(
            piece, piece, gather_s.at[turn, half, 0], gather_r.at[turn, half, dy * SIDE + dx], (row, col)
        ).wait_recv()

    def gather_forward(buf, turn, half, copies, d):
        arrived(buf, turn, half, turned(half, d, 0))
        for e in NEAR_FAR:
            forward(buf, turn, half, turned(half, d, 0), turned(half, 0, e), copies)

    def gather_end(buf, turn, half, copies):
        for e in NEAR_FAR:
            for d in range(SIDE):
                arrived(buf, turn, half, turned(half, d, e))
        for copy in copies:
            copy.wait_send()

    gathers = []
    for i in range(block_rows):
        if i == 5:
            pl.semaphore_wait(barrier, len(row_offsets) + len(COL_ORDER))
            gathers = [gather_start(first, 0, half) for half in range(2)]
        loads[i].wait()
        total = jnp.zeros((8, 256), F32)
        for s in range(slots):
            alive = jnp.where(s < counts[0, i], 1.0, 0.0).astype(F32)
            block = stored[i * slots + s].T
            stored[i * slots + s] = block
            total += jnp.sum(jnp.abs(block).astype(F32).reshape(32, 8, 256), axis=0) * alive
        deg_out[i // 2, i % 2] = jnp.sum(total, axis=0, keepdims=True)

    deg_copies = []
    for k, (dz, dc) in enumerate(COL_ORDER):
        to = column_of(dz, dc)
        deg_copies.append(send(deg_out.at[to], deg_in.at[k], deg_s.at[k], deg_r.at[k], (row, to)))
        deg_copies[-1].start()
    for d in NEAR_FAR:
        for half in range(2):
            gather_forward(first, 0, half, gathers[half], d)
    degree = deg_out[col]
    for k, copy in enumerate(deg_copies):
        copy.wait_recv()
        degree = degree + deg_in[k]
    own_scale[...] = 1.0 / jnp.sqrt(degree)
    scales[mine] = own_scale[...]
    scale_copies = []
    for k, (dy, dx) in enumerate(row_offsets):
        scale_copies.append(send(own_scale, scales.at[mine], scale_s.at[k], scale_r.at[k], (chip(dy, dx), col)))
        scale_copies[-1].start()
    for half in range(2):
        gather_end(first, 0, half, gathers[half])
    for k, (dy, dx) in enumerate(row_offsets):
        theirs = pl.ds(chip(SIDE - dy, SIDE - dx) * 2, 2)
        send(own_scale, scales.at[theirs], scale_s.at[k], scale_r.at[k], (row, col)).wait_recv()

    def scale_block(g, carry):
        first[g] = (first[g].astype(F32) * scales[g]).astype(BF16)
        return carry

    lax.fori_loop(0, 32, scale_block, 0, unroll=4)

    def product(buf, turn, half):
        started = []
        for k, (dz, dc) in enumerate(COL_ORDER + ((0, 0),)):
            to = column_of(dz, dc)
            i = to * 2 + half
            total = jnp.zeros((64, 256), F32)
            for s in range(slots):
                g = jnp.where(s < counts[0, i], columns[s, i], 32)
                total += jnp.dot(buf[g], stored[i * slots + s], preferred_element_type=F32)
            if k == len(COL_ORDER):
                part_own[half] = total
            else:
                part_out[turn, half, k] = total.astype(BF16)
                started.append(
                    send(
                        part_out.at[turn, half, k], part_in.at[turn, half, k], part_s.at[turn, half, k],
                        part_r.at[turn, half, k], (row, to),
                    )
                )
                started[-1].start()
        return started

    def summed(started, turn, half):
        total = part_own[half]
        for k, copy in enumerate(started):
            copy.wait_recv()
            total = total + part_in[turn, half, k].astype(F32)
        return total * own_scale[half]

    def local_gram(values):
        return lax.dot_general(values, values, NT, precision=HIGHEST, preferred_element_type=F32)

    parts = [product(first, 0, half) for half in range(2)]
    gathers, gram = [], jnp.zeros((64, 64), F32)
    for half in range(2):
        values = summed(parts[half], 0, half)
        second[row * 2 + half] = (values * own_scale[half]).astype(BF16)
        gathers.append(gather_start(second, 1, half))
        gram += local_gram(values)
    sent = parts[0] + parts[1] + deg_copies + scale_copies
    packed = pack(gram)
    for p in range(8):
        piece_out[p] = packed[p * 4 : (p + 1) * 4]
    piece_copies = []
    for k, (dz, dc) in enumerate(COL_ORDER):
        to = column_of(dz, dc)
        piece_copies.append(send(piece_out.at[to], piece_in.at[k], pa_s.at[k], pa_r.at[k], (row, to)))
        piece_copies[-1].start()
    for d in NEAR_FAR:
        gather_forward(second, 1, 0, gathers[0], d)
    for d in NEAR_FAR:
        gather_forward(second, 1, 1, gathers[1], d)
    total = piece_out[col]
    for k, copy in enumerate(piece_copies):
        copy.wait_recv()
        total = total + piece_in[k]
    piece_sum[0] = total
    across = []
    for k, (dy, dx) in enumerate(row_offsets):
        across.append(send(piece_sum.at[0], piece_row.at[k], pb_s.at[k], pb_r.at[k], (chip(dy, dx), col)))
        across[-1].start()
    sent += piece_copies + across
    for half in range(2):
        gather_end(second, 1, half, gathers[half])

    parts = [product(second, 1, 0)]
    for k, copy in enumerate(across):
        copy.wait_recv()
        total = total + piece_row[k]
    piece_sum[1] = total
    piece_all[col] = total
    back = []
    for k, (dz, dc) in enumerate(COL_ORDER):
        back.append(send(piece_sum.at[1], piece_all.at[col], pc_s.at[k], pc_r.at[k], (row, column_of(dz, dc))))
        back[-1].start()
    parts.append(product(second, 1, 1))
    for k, (dz, dc) in enumerate(COL_ORDER):
        source = piece_all.at[column_of(SIDE - dz, dc)]
        send(source, source, pc_s.at[k], pc_r.at[k], (row, col)).wait_recv()
    inverse = inverse_factor(unpack(jnp.concatenate([piece_all[p] for p in range(8)], axis=0)) / sites)
    gram = jnp.zeros((64, 64), F32)
    for half in range(2):
        values = jnp.dot(inverse, summed(parts[half], 1, half), precision=HIGHEST, preferred_element_type=F32)
        grown[half] = values
        gram += local_gram(values)
    sent += back + parts[0] + parts[1]

    gram_out[...] = pack(gram).astype(BF16)
    group = []
    for k, (dz, dc) in enumerate(COL_ORDER):
        group.append(send(gram_out, gram_in.at[k], ga_s.at[k], ga_r.at[k], (row, column_of(dz, dc))))
        group[-1].start()
    total = gram_out[...].astype(F32)
    for k, copy in enumerate(group):
        copy.wait_recv()
        total = total + gram_in[k].astype(F32)
    cross_out[...] = total.astype(BF16)
    across = []
    for k, (dy, dx) in enumerate(row_offsets):
        across.append(send(cross_out, cross_in.at[k], gb_s.at[k], gb_r.at[k], (chip(dy, dx), col)))
        across[-1].start()
    for copy in sent + group:
        copy.wait_send()
    total = cross_out[...].astype(F32)
    for k, copy in enumerate(across):
        copy.wait_recv()
        total = total + cross_in[k].astype(F32)
    inverse = inverse_factor(unpack(total) / sites)
    for half in range(2):
        out[:, half * 256 : (half + 1) * 256] = jnp.dot(
            inverse, grown[half], precision=HIGHEST, preferred_element_type=F32
        )
    for copy in across:
        copy.wait_send()


def per_device(panel, blocks, columns, counts):
    dma = pltpu.SemaphoreType.DMA
    return pl.pallas_call(
        kernel,
        out_shape=jax.ShapeDtypeStruct(panel.shape, F32),
        in_specs=[pl.BlockSpec(memory_space=pl.ANY)] * 4,
        out_specs=pl.BlockSpec(memory_space=pltpu.VMEM),
        scratch_shapes=[
            pltpu.VMEM((128, 256, 256), BF16),
            pltpu.VMEM((64, 512), F32),
            pltpu.SMEM((8, 16), jnp.int32),
            pltpu.SMEM((1, 16), jnp.int32),
            pltpu.VMEM((33, 64, 256), BF16),
            pltpu.VMEM((33, 64, 256), BF16),
            pltpu.VMEM((32, 1, 256), F32),
            pltpu.VMEM((2, 1, 256), F32),
            pltpu.VMEM((8, 2, 1, 256), F32),
            pltpu.VMEM((7, 2, 1, 256), F32),
            pltpu.VMEM((2, 2, 7, 64, 256), BF16),
            pltpu.VMEM((2, 2, 7, 64, 256), BF16),
            pltpu.VMEM((2, 64, 256), F32),
            pltpu.VMEM((8, 4, 128), F32),
            pltpu.VMEM((7, 4, 128), F32),
            pltpu.VMEM((2, 4, 128), F32),
            pltpu.VMEM((15, 4, 128), F32),
            pltpu.VMEM((8, 4, 128), F32),
            pltpu.VMEM((32, 128), BF16),
            pltpu.VMEM((7, 32, 128), BF16),
            pltpu.VMEM((32, 128), BF16),
            pltpu.VMEM((15, 32, 128), BF16),
            pltpu.VMEM((2, 64, 256), F32),
            dma((3,)),
            dma((16,)),
            dma((7,)),
            dma((7,)),
            dma((15,)),
            dma((15,)),
            dma((2, 2, 15)),
            dma((2, 2, 16)),
            dma((2, 2, 7)),
            dma((2, 2, 7)),
            dma((7,)),
            dma((7,)),
            dma((15,)),
            dma((15,)),
            dma((7,)),
            dma((7,)),
            dma((7,)),
            dma((7,)),
            dma((15,)),
            dma((15,)),
        ],
        compiler_params=pltpu.CompilerParams(
            collective_id=0, has_side_effects=True, vmem_limit_bytes=48 * 2**20
        ),
    )(panel, blocks, jnp.transpose(columns, (1, 2, 0)), jnp.transpose(counts))


def solution(mesh):
    in_specs = (
        P(None, ("row", "col")),
        P("row", "col", None, None, None),
        P("row", "col", None),
        P("row", "col"),
    )
    return jax.shard_map(
        per_device, mesh=mesh, in_specs=in_specs, out_specs=P(None, ("row", "col")), check_vma=False
    )
```

```python
import functools

import jax
import jax.numpy as jnp
from jax import lax
from jax.experimental import pallas as pl
from jax.experimental.pallas import tpu as pltpu
from jax.sharding import PartitionSpec as P

MESH = pl.DeviceIdType.MESH
HIGHEST = lax.Precision.HIGHEST
F32 = jnp.float32
BF16 = jnp.bfloat16
NT = (((1,), (1,)), ((), ()))
SIDE = 4
DEAD = 32
PANEL = 16

COL_ORDER = ((2, 0), (2, 1), (1, 0), (1, 1), (3, 0), (3, 1), (0, 1), (0, 0))
OTHERS = COL_ORDER[:-1]
Z_ORDER = (2, 1, 3)
FAR, NEAR = pl.ds(0, 3), pl.ds(3, 1)
NEAR_FAR = (1, 3, 2)


def inverse_factor(gram):
    size = gram.shape[0]
    rows = lax.broadcasted_iota(jnp.int32, (size, size), 0)
    lanes = lax.broadcasted_iota(jnp.int32, (size, size), 1)
    rest = jnp.concatenate([gram, (rows == lanes).astype(F32)], axis=1)
    done = []
    for first in range(0, size, PANEL):
        below = lax.broadcasted_iota(jnp.int32, rest.shape, 0)
        column = [jnp.broadcast_to(rest[:, first + q : first + q + 1], rest.shape) for q in range(PANEL)]
        pivots = []
        for q in range(PANEL):
            pivot = column[q][q : q + 1]
            pivots.append(pivot)
            factor = jnp.where(below > q, column[q] * (1.0 / pivot), 0.0)
            rest = rest - factor * rest[q : q + 1]
            for later in range(q + 1, PANEL):
                column[later] = column[later] - factor * column[later][q : q + 1]
        done.append(rest[:PANEL, size:] * lax.rsqrt(jnp.concatenate(pivots, axis=0)[:, size:]))
        rest = rest[PANEL:]
    return jnp.concatenate(done, axis=0)


def pack(gram):
    half = gram.shape[0] // 2
    return jnp.concatenate([gram[:half], gram[half:]], axis=1)


def unpack(packed):
    width = packed.shape[1] // 2
    return jnp.concatenate([packed[:, :width], packed[:, width:]], axis=0)


def kernel(
    panel, blocks, table_in, out,
    stored, start, table, first, second, scales, own_scale, deg_out, deg_in, pair_out, pair_in, far_out, far_in, part_own,
    piece_out, piece_in, piece_sum, piece_row, piece_all, gram_out, gram_in, cross_out, cross_in, grown,
    small_sem, load_sem, deg_s, deg_r, scale_s, scale_r, gather_s, gather_r, pair_s, pair_r, far_s, far_r,
    pa_s, pa_r, pb_s, pb_r, pc_s, pc_r, ga_s, ga_r, gb_s, gb_r,
):
    row, col = lax.axis_index("row"), lax.axis_index("col")
    y, x = row // SIDE, row % SIDE
    z, core = col // 2, col % 2
    slots, block_rows = table.shape
    sites = 65536

    def chip(dy, dx):
        return ((y + dy) % SIDE) * SIDE + (x + dx) % SIDE

    def column_of(dz, dc):
        return ((z + dz) % SIDE) * 2 + (core + dc) % 2

    def send(src, dst, send_sem, recv_sem, to):
        return pltpu.make_async_remote_copy(
            src_ref=src, dst_ref=dst, send_sem=send_sem, recv_sem=recv_sem, device_id=to, device_id_type=MESH
        )

    def arrivals(copies):
        for copy in copies:
            copy.wait_recv()

    small = [
        pltpu.make_async_copy(panel, start, small_sem.at[0]),
        pltpu.make_async_copy(table_in, table, small_sem.at[1]),
    ]
    loads = [
        pltpu.make_async_copy(blocks.at[i, 0], stored.at[pl.ds(i * slots, slots)], load_sem.at[i])
        for i in range(block_rows)
    ]
    for load in small + loads:
        load.start()

    barrier = pltpu.get_barrier_semaphore()
    row_offsets = [(dy, dx) for dy in (2, 1, 3, 0) for dx in (2, 1, 3, 0) if (dy, dx) != (0, 0)]
    for dy, dx in row_offsets:
        pl.semaphore_signal(barrier, inc=1, device_id=(chip(dy, dx), col), device_id_type=MESH)
    for dz, dc in OTHERS:
        pl.semaphore_signal(barrier, inc=1, device_id=(row, column_of(dz, dc)), device_id_type=MESH)

    mine = pl.ds(row * 2, 2)
    first[DEAD] = jnp.zeros_like(first[DEAD])
    second[DEAD] = jnp.zeros_like(second[DEAD])
    for load in small:
        load.wait()
    for half in range(2):
        first[row * 2 + half] = start[:, half * 256 : (half + 1) * 256].astype(BF16)

    def forward(buf, turn, half, src, to, copies):
        (sy, sx), (ty, tx) = src, to
        piece = chip(SIDE - sy, SIDE - sx) * 2 + half
        arrives = ((sy + ty) % SIDE) * SIDE + (sx + tx) % SIDE
        copies.append(
            send(
                buf.at[piece], buf.at[piece], gather_s.at[turn, half, len(copies)], gather_r.at[turn, half, arrives],
                (chip(ty, tx), col),
            )
        )
        copies[-1].start()

    def turned(half, one, other):
        return (other, one) if half == 0 else (one, other)

    def gather_start(buf, turn, half):
        copies = []
        for d in NEAR_FAR:
            forward(buf, turn, half, (0, 0), turned(half, d, 0), copies)
        for d in NEAR_FAR:
            forward(buf, turn, half, (0, 0), turned(half, 0, d), copies)
        return copies

    def arrived(buf, turn, half, offset):
        dy, dx = offset
        piece = buf.at[chip(SIDE - dy, SIDE - dx) * 2 + half]
        send(
            piece, piece, gather_s.at[turn, half, 0], gather_r.at[turn, half, dy * SIDE + dx], (row, col)
        ).wait_recv()

    def gather_forward(buf, turn, half, copies, d):
        arrived(buf, turn, half, turned(half, d, 0))
        for e in NEAR_FAR:
            forward(buf, turn, half, turned(half, d, 0), turned(half, 0, e), copies)

    def gather_end(buf, turn, half, copies):
        for e in NEAR_FAR:
            for d in range(SIDE):
                arrived(buf, turn, half, turned(half, d, e))
        for copy in copies:
            copy.wait_send()

    gathers = []
    for i in range(block_rows):
        if i == 5:
            pl.semaphore_wait(barrier, len(row_offsets) + len(OTHERS))
            gathers = [gather_start(first, 0, half) for half in range(2)]
        loads[i].wait()
        total = jnp.zeros((8, 256), F32)
        for s in range(slots):
            alive = jnp.where(table[s, i] < DEAD, 1.0, 0.0).astype(F32)
            block = stored[i * slots + s].T
            stored[i * slots + s] = block
            total += jnp.sum(jnp.abs(block).astype(F32).reshape(32, 8, 256), axis=0) * alive
        deg_out[i // 2, i % 2] = jnp.sum(total, axis=0, keepdims=True)

    deg_copies = []
    for k, (dz, dc) in enumerate(OTHERS):
        to = column_of(dz, dc)
        deg_copies.append(send(deg_out.at[to], deg_in.at[k], deg_s.at[k], deg_r.at[k], (row, to)))
        deg_copies[-1].start()
    for d in NEAR_FAR:
        for half in range(2):
            gather_forward(first, 0, half, gathers[half], d)
    arrivals(deg_copies)
    degree = sum((deg_in[k] for k in range(7)), deg_out[col])
    own_scale[...] = 1.0 / jnp.sqrt(degree)
    scales[mine] = own_scale[...]
    scale_copies = []
    for k, (dy, dx) in enumerate(row_offsets):
        scale_copies.append(send(own_scale, scales.at[mine], scale_s.at[k], scale_r.at[k], (chip(dy, dx), col)))
        scale_copies[-1].start()
    for half in range(2):
        gather_end(first, 0, half, gathers[half])
    for k, (dy, dx) in enumerate(row_offsets):
        theirs = pl.ds(chip(SIDE - dy, SIDE - dx) * 2, 2)
        send(own_scale, scales.at[theirs], scale_s.at[k], scale_r.at[k], (row, col)).wait_recv()

    def scale_block(g, carry):
        first[g] = (first[g].astype(F32) * scales[g]).astype(BF16)
        return carry

    lax.fori_loop(0, 32, scale_block, 0, unroll=4)

    def block_row(buf, i):
        total = jnp.zeros((64, 256), F32)
        for s in range(slots):
            total += jnp.dot(buf[table[s, i]], stored[i * slots + s], preferred_element_type=F32)
        return total

    def row_group(buf, wanted):
        return [block_row(buf, column_of(dz, dc) * 2 + half) for dz, dc, half in wanted]

    def to_other_core(turn, half, which):
        src, dst = pair_out.at[turn, half, which], pair_in.at[turn, half, which]
        k = 0 if which == FAR else 1
        copy = send(src, dst, pair_s.at[turn, half, k], pair_r.at[turn, half, k], (row, column_of(0, 1)))
        copy.start()
        return copy

    def product(buf, turn):
        pairs, fars = [], []
        for half in range(2):
            for k, total in enumerate(row_group(buf, [(dz, 1, half) for dz in Z_ORDER])):
                pair_out[turn, half, k] = total.astype(BF16)
            pairs.append(to_other_core(turn, half, FAR))
            totals = row_group(buf, [(dz, 0, half) for dz in Z_ORDER])
            pairs[half].wait_recv()
            for k, total in enumerate(totals):
                far_out[turn, half, k] = (total + pair_in[turn, half, k].astype(F32)).astype(BF16)
            fars.append([])
            for k, dz in enumerate(Z_ORDER):
                fars[half].append(
                    send(
                        far_out.at[turn, half, k], far_in.at[turn, half, k], far_s.at[turn, half, k],
                        far_r.at[turn, half, k], (row, column_of(dz, 0)),
                    )
                )
                fars[half][-1].start()
        totals = row_group(buf, [(0, 1, 0), (0, 1, 1), (0, 0, 0), (0, 0, 1)])
        for half in range(2):
            pair_out[turn, half, len(Z_ORDER)] = totals[half].astype(BF16)
            part_own[half] = totals[2 + half]
        near = [to_other_core(turn, half, NEAR) for half in range(2)]
        return [[near[half]] + fars[half] for half in range(2)], pairs + near + fars[0] + fars[1]

    def summed(started, turn, half):
        arrivals(started[half])
        total = part_own[half] + pair_in[turn, half, len(Z_ORDER)].astype(F32)
        for k in range(len(Z_ORDER)):
            total += far_in[turn, half, k].astype(F32)
        return total * own_scale[half]

    def local_gram(values):
        return lax.dot_general(values, values, NT, precision=HIGHEST, preferred_element_type=F32)

    parts, started = product(first, 0)
    gathers, gram = [], jnp.zeros((64, 64), F32)
    for half in range(2):
        values = summed(parts, 0, half)
        second[row * 2 + half] = (values * own_scale[half]).astype(BF16)
        gathers.append(gather_start(second, 1, half))
        gram += local_gram(values)
    sent = started + deg_copies + scale_copies
    packed = pack(gram)
    for p in range(8):
        piece_out[p] = packed[p * 4 : (p + 1) * 4]
    piece_copies = []
    for k, (dz, dc) in enumerate(OTHERS):
        to = column_of(dz, dc)
        piece_copies.append(send(piece_out.at[to], piece_in.at[k], pa_s.at[k], pa_r.at[k], (row, to)))
        piece_copies[-1].start()
    for d in NEAR_FAR:
        gather_forward(second, 1, 0, gathers[0], d)
    for d in NEAR_FAR:
        gather_forward(second, 1, 1, gathers[1], d)
    arrivals(piece_copies)
    piece_sum[0] = sum((piece_in[k] for k in range(7)), piece_out[col])
    across = []
    for k, (dy, dx) in enumerate(row_offsets):
        across.append(send(piece_sum.at[0], piece_row.at[k], pb_s.at[k], pb_r.at[k], (chip(dy, dx), col)))
        across[-1].start()
    sent += piece_copies + across
    for half in range(2):
        gather_end(second, 1, half, gathers[half])

    arrivals(across)
    total = sum((piece_row[k] for k in range(15)), piece_sum[0])
    piece_sum[1] = total
    piece_all[col] = total
    back = []
    for k, (dz, dc) in enumerate(OTHERS):
        back.append(send(piece_sum.at[1], piece_all.at[col], pc_s.at[k], pc_r.at[k], (row, column_of(dz, dc))))
        back[-1].start()
    parts, started = product(second, 1)
    for k, (dz, dc) in enumerate(OTHERS):
        source = piece_all.at[column_of(SIDE - dz, dc)]
        send(source, source, pc_s.at[k], pc_r.at[k], (row, col)).wait_recv()
    inverse = inverse_factor(unpack(jnp.concatenate([piece_all[p] for p in range(8)], axis=0)) / sites)
    gram = jnp.zeros((64, 64), F32)
    for half in range(2):
        values = jnp.dot(inverse, summed(parts, 1, half), precision=HIGHEST, preferred_element_type=F32)
        grown[half] = values
        gram += local_gram(values)
    sent += back + started

    gram_out[...] = pack(gram).astype(BF16)
    group = []
    for k, (dz, dc) in enumerate(OTHERS):
        group.append(send(gram_out, gram_in.at[k], ga_s.at[k], ga_r.at[k], (row, column_of(dz, dc))))
        group[-1].start()
    arrivals(group)
    total = sum((gram_in[k].astype(F32) for k in range(7)), gram_out[...].astype(F32))
    cross_out[...] = total.astype(BF16)
    across = []
    for k, (dy, dx) in enumerate(row_offsets):
        across.append(send(cross_out, cross_in.at[k], gb_s.at[k], gb_r.at[k], (chip(dy, dx), col)))
        across[-1].start()
    for copy in sent + group:
        copy.wait_send()
    arrivals(across)
    total = sum((cross_in[k].astype(F32) for k in range(15)), cross_out[...].astype(F32))
    inverse = inverse_factor(unpack(total) / sites)
    for half in range(2):
        out[:, half * 256 : (half + 1) * 256] = jnp.dot(
            inverse, grown[half], precision=HIGHEST, preferred_element_type=F32
        )
    for copy in across:
        copy.wait_send()


def per_device(panel, blocks, columns, counts):
    live = jnp.arange(columns.shape[2], dtype=jnp.int32)[:, None] < jnp.transpose(counts)
    table = jnp.where(live, jnp.transpose(columns[:, 0]), DEAD)
    dma = pltpu.SemaphoreType.DMA
    return pl.pallas_call(
        kernel,
        out_shape=jax.ShapeDtypeStruct(panel.shape, F32),
        in_specs=[pl.BlockSpec(memory_space=pl.ANY)] * 3,
        out_specs=pl.BlockSpec(memory_space=pltpu.VMEM),
        scratch_shapes=[
            pltpu.VMEM((128, 256, 256), BF16),
            pltpu.VMEM((64, 512), F32),
            pltpu.SMEM((8, 16), jnp.int32),
            pltpu.VMEM((33, 64, 256), BF16),
            pltpu.VMEM((33, 64, 256), BF16),
            pltpu.VMEM((32, 1, 256), F32),
            pltpu.VMEM((2, 1, 256), F32),
            pltpu.VMEM((8, 2, 1, 256), F32),
            pltpu.VMEM((7, 2, 1, 256), F32),
            pltpu.VMEM((2, 2, 4, 64, 256), BF16),
            pltpu.VMEM((2, 2, 4, 64, 256), BF16),
            pltpu.VMEM((2, 2, 3, 64, 256), BF16),
            pltpu.VMEM((2, 2, 3, 64, 256), BF16),
            pltpu.VMEM((2, 64, 256), F32),
            pltpu.VMEM((8, 4, 128), F32),
            pltpu.VMEM((7, 4, 128), F32),
            pltpu.VMEM((2, 4, 128), F32),
            pltpu.VMEM((15, 4, 128), F32),
            pltpu.VMEM((8, 4, 128), F32),
            pltpu.VMEM((32, 128), BF16),
            pltpu.VMEM((7, 32, 128), BF16),
            pltpu.VMEM((32, 128), BF16),
            pltpu.VMEM((15, 32, 128), BF16),
            pltpu.VMEM((2, 64, 256), F32),
            dma((2,)),
            dma((16,)),
            dma((7,)),
            dma((7,)),
            dma((15,)),
            dma((15,)),
            dma((2, 2, 15)),
            dma((2, 2, 16)),
            dma((2, 2, 2)),
            dma((2, 2, 2)),
            dma((2, 2, 3)),
            dma((2, 2, 3)),
            dma((7,)),
            dma((7,)),
            dma((15,)),
            dma((15,)),
            dma((7,)),
            dma((7,)),
            dma((7,)),
            dma((7,)),
            dma((15,)),
            dma((15,)),
        ],
        compiler_params=pltpu.CompilerParams(
            collective_id=0, has_side_effects=True, vmem_limit_bytes=48 * 2**20
        ),
    )(panel, blocks, table)


def solution(mesh):
    in_specs = (
        P(None, ("row", "col")),
        P("row", "col", None, None, None),
        P("row", "col", None),
        P("row", "col"),
    )
    return jax.shard_map(
        per_device, mesh=mesh, in_specs=in_specs, out_specs=P(None, ("row", "col")), check_vma=False
    )
```

```python
import functools

import jax
import jax.numpy as jnp
from jax import lax
from jax.experimental import pallas as pl
from jax.experimental.pallas import tpu as pltpu
from jax.sharding import PartitionSpec as P

MESH = pl.DeviceIdType.MESH
HIGHEST = lax.Precision.HIGHEST
F32 = jnp.float32
BF16 = jnp.bfloat16
NT = (((1,), (1,)), ((), ()))
SIDE = 4
DEAD = 32
PANEL = 16

COL_ORDER = ((2, 0), (2, 1), (1, 0), (1, 1), (3, 0), (3, 1), (0, 1), (0, 0))
OTHERS = COL_ORDER[:-1]
Z_ORDER = (2, 1, 3)
FAR, NEAR = pl.ds(0, 3), pl.ds(3, 1)
NEAR_FAR = (1, 3, 2)
PARTS = (1, 2)


def inverse_factor(gram):
    size = gram.shape[0]
    rows = lax.broadcasted_iota(jnp.int32, (size, size), 0)
    lanes = lax.broadcasted_iota(jnp.int32, (size, size), 1)
    rest = jnp.concatenate([gram, (rows == lanes).astype(F32)], axis=1)
    done = []
    for first in range(0, size, PANEL):
        below = lax.broadcasted_iota(jnp.int32, rest.shape, 0)
        column = [jnp.broadcast_to(rest[:, first + q : first + q + 1], rest.shape) for q in range(PANEL)]
        pivots = []
        for q in range(PANEL):
            pivot = column[q][q : q + 1]
            pivots.append(pivot)
            factor = jnp.where(below > q, column[q] * (1.0 / pivot), 0.0)
            rest = rest - factor * rest[q : q + 1]
            for later in range(q + 1, PANEL):
                column[later] = column[later] - factor * column[later][q : q + 1]
        done.append(rest[:PANEL, size:] * lax.rsqrt(jnp.concatenate(pivots, axis=0)[:, size:]))
        rest = rest[PANEL:]
    return jnp.concatenate(done, axis=0)


def pack(gram):
    half = gram.shape[0] // 2
    return jnp.concatenate([gram[:half], gram[half:]], axis=1)


def unpack(packed):
    width = packed.shape[1] // 2
    return jnp.concatenate([packed[:, :width], packed[:, width:]], axis=0)


def kernel(
    panel, blocks, table_in, out,
    stored, start, table, first, second, scales, own_scale, deg_out, deg_in, pair_out, pair_in, far_out, far_in, part_own,
    gram_out, gram_in, cross_out, cross_in, grown,
    small_sem, load_sem, deg_s, deg_r, scale_s, scale_r, gather_s, gather_r, pair_s, pair_r, far_s, far_r,
    ga_s, ga_r, gb_s, gb_r,
):
    row, col = lax.axis_index("row"), lax.axis_index("col")
    y, x = row // SIDE, row % SIDE
    z, core = col // 2, col % 2
    slots, block_rows = table.shape
    sites = 65536

    def chip(dy, dx):
        return ((y + dy) % SIDE) * SIDE + (x + dx) % SIDE

    def column_of(dz, dc):
        return ((z + dz) % SIDE) * 2 + (core + dc) % 2

    def send(src, dst, send_sem, recv_sem, to):
        return pltpu.make_async_remote_copy(
            src_ref=src, dst_ref=dst, send_sem=send_sem, recv_sem=recv_sem, device_id=to, device_id_type=MESH
        )

    def arrivals(copies):
        for copy in copies:
            copy.wait_recv()

    small = [
        pltpu.make_async_copy(panel, start, small_sem.at[0]),
        pltpu.make_async_copy(table_in, table, small_sem.at[1]),
    ]
    loads = [
        pltpu.make_async_copy(blocks.at[i, 0], stored.at[pl.ds(i * slots, slots)], load_sem.at[i])
        for i in range(block_rows)
    ]
    for load in small + loads:
        load.start()

    barrier = pltpu.get_barrier_semaphore()
    row_offsets = [(dy, dx) for dy in (2, 1, 3, 0) for dx in (2, 1, 3, 0) if (dy, dx) != (0, 0)]
    for dy, dx in row_offsets:
        pl.semaphore_signal(barrier, inc=1, device_id=(chip(dy, dx), col), device_id_type=MESH)
    for dz, dc in OTHERS:
        pl.semaphore_signal(barrier, inc=1, device_id=(row, column_of(dz, dc)), device_id_type=MESH)

    mine = pl.ds(row * 2, 2)
    first[DEAD] = jnp.zeros_like(first[DEAD])
    second[DEAD] = jnp.zeros_like(second[DEAD])
    for load in small:
        load.wait()
    for half in range(2):
        first[row * 2 + half] = start[:, half * 256 : (half + 1) * 256].astype(BF16)

    def vectors(turn, part):
        size = 64 // PARTS[turn]
        return pl.ds(part * size, size)

    def forward(buf, turn, half, part, src, to, copies):
        (sy, sx), (ty, tx) = src, to
        piece = buf.at[chip(SIDE - sy, SIDE - sx) * 2 + half, vectors(turn, part)]
        arrives = ((sy + ty) % SIDE) * SIDE + (sx + tx) % SIDE
        copies.append(
            send(
                piece, piece, gather_s.at[turn, half, len(copies)], gather_r.at[turn, half, part, arrives],
                (chip(ty, tx), col),
            )
        )
        copies[-1].start()

    def turned(turn, half, part, one, other):
        along_x = half == 0 if PARTS[turn] == 1 else part % 2 == 0
        return (other, one) if along_x else (one, other)

    def gather_start(buf, turn, half):
        copies = []
        for d in NEAR_FAR:
            for part in range(PARTS[turn]):
                forward(buf, turn, half, part, (0, 0), turned(turn, half, part, d, 0), copies)
        for d in NEAR_FAR:
            for part in range(PARTS[turn]):
                forward(buf, turn, half, part, (0, 0), turned(turn, half, part, 0, d), copies)
        return copies

    def arrived(buf, turn, half, part, offset):
        dy, dx = offset
        piece = buf.at[chip(SIDE - dy, SIDE - dx) * 2 + half, vectors(turn, part)]
        send(
            piece, piece, gather_s.at[turn, half, 0], gather_r.at[turn, half, part, dy * SIDE + dx], (row, col)
        ).wait_recv()

    def gather_forward(buf, turn, half, copies, d):
        for part in range(PARTS[turn]):
            arrived(buf, turn, half, part, turned(turn, half, part, d, 0))
            for e in NEAR_FAR:
                forward(buf, turn, half, part, turned(turn, half, part, d, 0), turned(turn, half, part, 0, e), copies)

    def gather_end(buf, turn, half, copies):
        for e in NEAR_FAR:
            for d in range(SIDE):
                for part in range(PARTS[turn]):
                    arrived(buf, turn, half, part, turned(turn, half, part, d, e))
        for copy in copies:
            copy.wait_send()

    gathers = []
    for i in range(block_rows):
        if i == 5:
            pl.semaphore_wait(barrier, len(row_offsets) + len(OTHERS))
            gathers = [gather_start(first, 0, half) for half in range(2)]
        loads[i].wait()
        total = jnp.zeros((8, 256), F32)
        for s in range(slots):
            alive = jnp.where(table[s, i] < DEAD, 1.0, 0.0).astype(F32)
            block = stored[i * slots + s].T
            stored[i * slots + s] = block
            total += jnp.sum(jnp.abs(block).astype(F32).reshape(32, 8, 256), axis=0) * alive
        deg_out[i // 2, i % 2] = jnp.sum(total, axis=0, keepdims=True)

    deg_copies = []
    for k, (dz, dc) in enumerate(OTHERS):
        to = column_of(dz, dc)
        deg_copies.append(send(deg_out.at[to], deg_in.at[k], deg_s.at[k], deg_r.at[k], (row, to)))
        deg_copies[-1].start()
    for d in NEAR_FAR:
        for half in range(2):
            gather_forward(first, 0, half, gathers[half], d)
    arrivals(deg_copies)
    degree = sum((deg_in[k] for k in range(7)), deg_out[col])
    own_scale[...] = 1.0 / jnp.sqrt(degree)
    scales[mine] = own_scale[...]
    scale_copies = []
    for k, (dy, dx) in enumerate(row_offsets):
        scale_copies.append(send(own_scale, scales.at[mine], scale_s.at[k], scale_r.at[k], (chip(dy, dx), col)))
        scale_copies[-1].start()
    for half in range(2):
        gather_end(first, 0, half, gathers[half])
    for k, (dy, dx) in enumerate(row_offsets):
        theirs = pl.ds(chip(SIDE - dy, SIDE - dx) * 2, 2)
        send(own_scale, scales.at[theirs], scale_s.at[k], scale_r.at[k], (row, col)).wait_recv()

    def scale_block(g, carry):
        first[g] = (first[g].astype(F32) * scales[g]).astype(BF16)
        return carry

    lax.fori_loop(0, 32, scale_block, 0, unroll=4)

    def block_row(buf, i):
        total = jnp.zeros((64, 256), F32)
        for s in range(slots):
            total += jnp.dot(buf[table[s, i]], stored[i * slots + s], preferred_element_type=F32)
        return total

    def row_group(buf, wanted):
        return [block_row(buf, column_of(dz, dc) * 2 + half) for dz, dc, half in wanted]

    def to_other_core(turn, half, which):
        src, dst = pair_out.at[turn, half, which], pair_in.at[turn, half, which]
        k = 0 if which == FAR else 1
        copy = send(src, dst, pair_s.at[turn, half, k], pair_r.at[turn, half, k], (row, column_of(0, 1)))
        copy.start()
        return copy

    def product(buf, turn):
        pairs, fars = [], []
        for half in range(2):
            for k, total in enumerate(row_group(buf, [(dz, 1, half) for dz in Z_ORDER])):
                pair_out[turn, half, k] = total.astype(BF16)
            pairs.append(to_other_core(turn, half, FAR))
            totals = row_group(buf, [(dz, 0, half) for dz in Z_ORDER])
            pairs[half].wait_recv()
            for k, total in enumerate(totals):
                far_out[turn, half, k] = (total + pair_in[turn, half, k].astype(F32)).astype(BF16)
            fars.append([])
            for k, dz in enumerate(Z_ORDER):
                fars[half].append(
                    send(
                        far_out.at[turn, half, k], far_in.at[turn, half, k], far_s.at[turn, half, k],
                        far_r.at[turn, half, k], (row, column_of(dz, 0)),
                    )
                )
                fars[half][-1].start()
        totals = row_group(buf, [(0, 1, 0), (0, 1, 1), (0, 0, 0), (0, 0, 1)])
        for half in range(2):
            pair_out[turn, half, len(Z_ORDER)] = totals[half].astype(BF16)
            part_own[half] = totals[2 + half]
        near = [to_other_core(turn, half, NEAR) for half in range(2)]
        return [[near[half]] + fars[half] for half in range(2)], pairs + near + fars[0] + fars[1]

    def summed(started, turn, half):
        arrivals(started[half])
        total = part_own[half] + pair_in[turn, half, len(Z_ORDER)].astype(F32)
        for k in range(len(Z_ORDER)):
            total += far_in[turn, half, k].astype(F32)
        return total * own_scale[half]

    def local_gram(values):
        return lax.dot_general(values, values, NT, precision=HIGHEST, preferred_element_type=F32)

    def gram_to_group(gram, turn):
        gram_out[turn] = pack(gram).astype(BF16)
        copies = []
        for k, (dz, dc) in enumerate(OTHERS):
            copies.append(
                send(
                    gram_out.at[turn], gram_in.at[turn, k], ga_s.at[turn, k], ga_r.at[turn, k],
                    (row, column_of(dz, dc)),
                )
            )
            copies[-1].start()
        return copies

    def gram_across(group, turn):
        arrivals(group)
        total = sum((gram_in[turn, k].astype(F32) for k in range(7)), gram_out[turn].astype(F32))
        cross_out[turn] = total.astype(BF16)
        copies = []
        for k, (dy, dx) in enumerate(row_offsets):
            copies.append(
                send(cross_out.at[turn], cross_in.at[turn, k], gb_s.at[turn, k], gb_r.at[turn, k], (chip(dy, dx), col))
            )
            copies[-1].start()
        return copies

    def gram_factor(across, turn):
        arrivals(across)
        total = sum((cross_in[turn, k].astype(F32) for k in range(15)), cross_out[turn].astype(F32))
        return inverse_factor(unpack(total) / sites)

    parts, started = product(first, 0)
    gathers, gram = [], jnp.zeros((64, 64), F32)
    for half in range(2):
        values = summed(parts, 0, half)
        second[row * 2 + half] = (values * own_scale[half]).astype(BF16)
        gathers.append(gather_start(second, 1, half))
        gram += local_gram(values)
    sent = started + deg_copies + scale_copies
    group = gram_to_group(gram, 0)
    gather_forward(second, 1, 0, gathers[0], NEAR_FAR[0])
    gather_forward(second, 1, 0, gathers[0], NEAR_FAR[1])
    gather_forward(second, 1, 1, gathers[1], NEAR_FAR[0])
    gather_forward(second, 1, 0, gathers[0], NEAR_FAR[2])
    gather_forward(second, 1, 1, gathers[1], NEAR_FAR[1])
    gather_forward(second, 1, 1, gathers[1], NEAR_FAR[2])
    for half in range(2):
        gather_end(second, 1, half, gathers[half])
    across = gram_across(group, 0)
    sent += group + across

    parts, started = product(second, 1)
    inverse = gram_factor(across, 0)
    gram = jnp.zeros((64, 64), F32)
    for half in range(2):
        values = jnp.dot(inverse, summed(parts, 1, half), precision=HIGHEST, preferred_element_type=F32)
        grown[half] = values
        gram += local_gram(values)
    sent += started

    group = gram_to_group(gram, 1)
    across = gram_across(group, 1)
    for copy in sent + group:
        copy.wait_send()
    inverse = gram_factor(across, 1)
    for half in range(2):
        out[:, half * 256 : (half + 1) * 256] = jnp.dot(
            inverse, grown[half], precision=HIGHEST, preferred_element_type=F32
        )
    for copy in across:
        copy.wait_send()


def per_device(panel, blocks, columns, counts):
    live = jnp.arange(columns.shape[2], dtype=jnp.int32)[:, None] < jnp.transpose(counts)
    table = jnp.where(live, jnp.transpose(columns[:, 0]), DEAD)
    dma = pltpu.SemaphoreType.DMA
    return pl.pallas_call(
        kernel,
        out_shape=jax.ShapeDtypeStruct(panel.shape, F32),
        in_specs=[pl.BlockSpec(memory_space=pl.ANY)] * 3,
        out_specs=pl.BlockSpec(memory_space=pltpu.VMEM),
        scratch_shapes=[
            pltpu.VMEM((128, 256, 256), BF16),
            pltpu.VMEM((64, 512), F32),
            pltpu.SMEM((8, 16), jnp.int32),
            pltpu.VMEM((33, 64, 256), BF16),
            pltpu.VMEM((33, 64, 256), BF16),
            pltpu.VMEM((32, 1, 256), F32),
            pltpu.VMEM((2, 1, 256), F32),
            pltpu.VMEM((8, 2, 1, 256), F32),
            pltpu.VMEM((7, 2, 1, 256), F32),
            pltpu.VMEM((2, 2, 4, 64, 256), BF16),
            pltpu.VMEM((2, 2, 4, 64, 256), BF16),
            pltpu.VMEM((2, 2, 3, 64, 256), BF16),
            pltpu.VMEM((2, 2, 3, 64, 256), BF16),
            pltpu.VMEM((2, 64, 256), F32),
            pltpu.VMEM((2, 32, 128), BF16),
            pltpu.VMEM((2, 7, 32, 128), BF16),
            pltpu.VMEM((2, 32, 128), BF16),
            pltpu.VMEM((2, 15, 32, 128), BF16),
            pltpu.VMEM((2, 64, 256), F32),
            dma((2,)),
            dma((16,)),
            dma((7,)),
            dma((7,)),
            dma((15,)),
            dma((15,)),
            dma((2, 2, 30)),
            dma((2, 2, 2, 16)),
            dma((2, 2, 2)),
            dma((2, 2, 2)),
            dma((2, 2, 3)),
            dma((2, 2, 3)),
            dma((2, 7)),
            dma((2, 7)),
            dma((2, 15)),
            dma((2, 15)),
        ],
        compiler_params=pltpu.CompilerParams(
            collective_id=0, has_side_effects=True, vmem_limit_bytes=48 * 2**20
        ),
    )(panel, blocks, table)


def solution(mesh):
    in_specs = (
        P(None, ("row", "col")),
        P("row", "col", None, None, None),
        P("row", "col", None),
        P("row", "col"),
    )
    return jax.shard_map(
        per_device, mesh=mesh, in_specs=in_specs, out_specs=P(None, ("row", "col")), check_vma=False
    )
```

```python
import functools

import jax
import jax.numpy as jnp
from jax import lax
from jax.experimental import pallas as pl
from jax.experimental.pallas import tpu as pltpu
from jax.sharding import PartitionSpec as P

MESH = pl.DeviceIdType.MESH
HIGHEST = lax.Precision.HIGHEST
F32 = jnp.float32
BF16 = jnp.bfloat16
NT = (((1,), (1,)), ((), ()))
SIDE = 4
ENTRY = 5
DEAD = 32
PANEL = 16

COL_ORDER = ((2, 0), (2, 1), (1, 0), (1, 1), (3, 0), (3, 1), (0, 1), (0, 0))
OTHERS = COL_ORDER[:-1]
Z_ORDER = (2, 1, 3)
FAR, NEAR = pl.ds(0, 3), pl.ds(3, 1)
NEAR_FAR = (1, 3, 2)
PARTS = (1, 2)


def inverse_factor(gram):
    size = gram.shape[0]
    rows = lax.broadcasted_iota(jnp.int32, (size, size), 0)
    lanes = lax.broadcasted_iota(jnp.int32, (size, size), 1)
    rest = jnp.concatenate([gram, (rows == lanes).astype(F32)], axis=1)
    done = []
    for first in range(0, size, PANEL):
        below = lax.broadcasted_iota(jnp.int32, rest.shape, 0)
        column = [jnp.broadcast_to(rest[:, first + q : first + q + 1], rest.shape) for q in range(PANEL)]
        pivots = []
        for q in range(PANEL):
            pivot = column[q][q : q + 1]
            pivots.append(pivot)
            factor = jnp.where(below > q, column[q] * (1.0 / pivot), 0.0)
            rest = rest - factor * rest[q : q + 1]
            for later in range(q + 1, PANEL):
                column[later] = column[later] - factor * column[later][q : q + 1]
        done.append(rest[:PANEL, size:] * lax.rsqrt(jnp.concatenate(pivots, axis=0)[:, size:]))
        rest = rest[PANEL:]
    return jnp.concatenate(done, axis=0)


def pack(gram):
    half = gram.shape[0] // 2
    return jnp.concatenate([gram[:half], gram[half:]], axis=1)


def unpack(packed):
    width = packed.shape[1] // 2
    return jnp.concatenate([packed[:, :width], packed[:, width:]], axis=0)


def kernel(
    panel, blocks, table_in, out,
    stored, start, table, first, second, scales, own_scale, deg_out, deg_in, pair_out, pair_in, far_out, far_in, part_own,
    gram_out, gram_in, cross_out, cross_in, grown,
    small_sem, load_sem, deg_s, deg_r, scale_s, scale_r, gather_s, gather_r, pair_s, pair_r, far_s, far_r,
    ga_s, ga_r, gb_s, gb_r,
):
    row, col = lax.axis_index("row"), lax.axis_index("col")
    y, x = row // SIDE, row % SIDE
    z, core = col // 2, col % 2
    slots = table.shape[0]
    sites = 65536

    def chip(dy, dx):
        return ((y + dy) % SIDE) * SIDE + (x + dx) % SIDE

    def column_of(dz, dc):
        return ((z + dz) % SIDE) * 2 + (core + dc) % 2

    def send(src, dst, send_sem, recv_sem, to):
        return pltpu.make_async_remote_copy(
            src_ref=src, dst_ref=dst, send_sem=send_sem, recv_sem=recv_sem, device_id=to, device_id_type=MESH
        )

    def arrivals(copies):
        for copy in copies:
            copy.wait_recv()

    small = [
        pltpu.make_async_copy(panel, start, small_sem.at[0]),
        pltpu.make_async_copy(table_in, table, small_sem.at[1]),
    ]
    by_owner = [column_of(dz, dc) * 2 + half for dz, dc in COL_ORDER for half in range(2)]
    loads = [
        pltpu.make_async_copy(blocks.at[i, 0], stored.at[pl.ds(i * slots, slots)], load_sem.at[n])
        for n, i in enumerate(by_owner)
    ]
    for load in small + loads:
        load.start()

    barrier = pltpu.get_barrier_semaphore()
    row_offsets = [(dy, dx) for dy in (2, 1, 3, 0) for dx in (2, 1, 3, 0) if (dy, dx) != (0, 0)]
    for dy, dx in row_offsets:
        pl.semaphore_signal(barrier, inc=1, device_id=(chip(dy, dx), col), device_id_type=MESH)
    for dz, dc in OTHERS:
        pl.semaphore_signal(barrier, inc=1, device_id=(row, column_of(dz, dc)), device_id_type=MESH)

    mine = pl.ds(row * 2, 2)
    first[DEAD] = jnp.zeros_like(first[DEAD])
    second[DEAD] = jnp.zeros_like(second[DEAD])
    for load in small:
        load.wait()
    for half in range(2):
        first[row * 2 + half] = start[:, half * 256 : (half + 1) * 256].astype(BF16)

    def vectors(turn, part):
        size = 64 // PARTS[turn]
        return pl.ds(part * size, size)

    def forward(buf, turn, half, part, src, to, copies):
        (sy, sx), (ty, tx) = src, to
        piece = buf.at[chip(SIDE - sy, SIDE - sx) * 2 + half, vectors(turn, part)]
        arrives = ((sy + ty) % SIDE) * SIDE + (sx + tx) % SIDE
        copies.append(
            send(
                piece, piece, gather_s.at[turn, half, len(copies)], gather_r.at[turn, half, part, arrives],
                (chip(ty, tx), col),
            )
        )
        copies[-1].start()

    def turned(turn, half, part, one, other):
        along_x = half == 0 if PARTS[turn] == 1 else part % 2 == 0
        return (other, one) if along_x else (one, other)

    def gather_start(buf, turn, half):
        copies = []
        for d in NEAR_FAR:
            for part in range(PARTS[turn]):
                forward(buf, turn, half, part, (0, 0), turned(turn, half, part, d, 0), copies)
        for d in NEAR_FAR:
            for part in range(PARTS[turn]):
                forward(buf, turn, half, part, (0, 0), turned(turn, half, part, 0, d), copies)
        return copies

    def arrived(buf, turn, half, part, offset):
        dy, dx = offset
        piece = buf.at[chip(SIDE - dy, SIDE - dx) * 2 + half, vectors(turn, part)]
        send(
            piece, piece, gather_s.at[turn, half, 0], gather_r.at[turn, half, part, dy * SIDE + dx], (row, col)
        ).wait_recv()

    def gather_forward(buf, turn, half, copies, d):
        for part in range(PARTS[turn]):
            arrived(buf, turn, half, part, turned(turn, half, part, d, 0))
            for e in NEAR_FAR:
                forward(buf, turn, half, part, turned(turn, half, part, d, 0), turned(turn, half, part, 0, e), copies)

    def gather_end(buf, turn, half, copies):
        for e in NEAR_FAR:
            for d in range(SIDE):
                for part in range(PARTS[turn]):
                    arrived(buf, turn, half, part, turned(turn, half, part, d, e))
        for copy in copies:
            copy.wait_send()

    gathers, deg_copies, begun = [], [], 0
    for n, i in enumerate(by_owner):
        if n == ENTRY:
            pl.semaphore_wait(barrier, len(row_offsets) + len(OTHERS))
            gathers = [gather_start(first, 0, half) for half in range(2)]
        loads[n].wait()
        total = jnp.zeros((8, 256), F32)
        for s in range(slots):
            alive = jnp.where(table[s, i] < DEAD, 1.0, 0.0).astype(F32)
            block = stored[i * slots + s].T
            stored[i * slots + s] = block
            total += jnp.sum(jnp.abs(block).astype(F32).reshape(32, 8, 256), axis=0) * alive
        deg_out[n // 2, n % 2] = jnp.sum(total, axis=0, keepdims=True)
        if n % 2 == 1 and n // 2 < len(OTHERS):
            k = n // 2
            deg_copies.append(
                send(deg_out.at[k], deg_in.at[k], deg_s.at[k], deg_r.at[k], (row, column_of(*COL_ORDER[k])))
            )
        if n >= ENTRY:
            for copy in deg_copies[begun:]:
                copy.start()
            begun = len(deg_copies)

    for d in NEAR_FAR[:2]:
        for half in range(2):
            gather_forward(first, 0, half, gathers[half], d)
    arrivals(deg_copies)
    degree = sum((deg_in[k] for k in range(7)), deg_out[7])
    own_scale[...] = 1.0 / jnp.sqrt(degree)
    scales[mine] = own_scale[...]
    scale_copies = []
    for k, (dy, dx) in enumerate(row_offsets):
        scale_copies.append(send(own_scale, scales.at[mine], scale_s.at[k], scale_r.at[k], (chip(dy, dx), col)))
        scale_copies[-1].start()
    for d in NEAR_FAR[2:]:
        for half in range(2):
            gather_forward(first, 0, half, gathers[half], d)
    for half in range(2):
        gather_end(first, 0, half, gathers[half])
    for k, (dy, dx) in enumerate(row_offsets):
        theirs = pl.ds(chip(SIDE - dy, SIDE - dx) * 2, 2)
        send(own_scale, scales.at[theirs], scale_s.at[k], scale_r.at[k], (row, col)).wait_recv()

    def scale_block(g, carry):
        first[g] = (first[g].astype(F32) * scales[g]).astype(BF16)
        return carry

    lax.fori_loop(0, 32, scale_block, 0, unroll=4)

    def block_row(buf, i):
        total = jnp.zeros((64, 256), F32)
        for s in range(slots):
            total += jnp.dot(buf[table[s, i]], stored[i * slots + s], preferred_element_type=F32)
        return total

    def row_group(buf, wanted):
        return [block_row(buf, column_of(dz, dc) * 2 + half) for dz, dc, half in wanted]

    def to_other_core(turn, half, which):
        src, dst = pair_out.at[turn, half, which], pair_in.at[turn, half, which]
        k = 0 if which == FAR else 1
        copy = send(src, dst, pair_s.at[turn, half, k], pair_r.at[turn, half, k], (row, column_of(0, 1)))
        copy.start()
        return copy

    def product(buf, turn):
        pairs, fars = [], []
        for half in range(2):
            for k, total in enumerate(row_group(buf, [(dz, 1, half) for dz in Z_ORDER])):
                pair_out[turn, half, k] = total.astype(BF16)
            pairs.append(to_other_core(turn, half, FAR))
            totals = row_group(buf, [(dz, 0, half) for dz in Z_ORDER])
            pairs[half].wait_recv()
            for k, total in enumerate(totals):
                far_out[turn, half, k] = (total + pair_in[turn, half, k].astype(F32)).astype(BF16)
            fars.append([])
            for k, dz in enumerate(Z_ORDER):
                fars[half].append(
                    send(
                        far_out.at[turn, half, k], far_in.at[turn, half, k], far_s.at[turn, half, k],
                        far_r.at[turn, half, k], (row, column_of(dz, 0)),
                    )
                )
                fars[half][-1].start()
        totals = row_group(buf, [(0, 1, 0), (0, 1, 1), (0, 0, 0), (0, 0, 1)])
        for half in range(2):
            pair_out[turn, half, len(Z_ORDER)] = totals[half].astype(BF16)
            part_own[half] = totals[2 + half]
        near = [to_other_core(turn, half, NEAR) for half in range(2)]
        return [[near[half]] + fars[half] for half in range(2)], pairs + near + fars[0] + fars[1]

    def summed(started, turn, half):
        arrivals(started[half])
        total = part_own[half] + pair_in[turn, half, len(Z_ORDER)].astype(F32)
        for k in range(len(Z_ORDER)):
            total += far_in[turn, half, k].astype(F32)
        return total * own_scale[half]

    def local_gram(values):
        return lax.dot_general(values, values, NT, precision=HIGHEST, preferred_element_type=F32)

    def gram_to_group(gram, turn):
        gram_out[turn] = pack(gram).astype(BF16)
        copies = []
        for k, (dz, dc) in enumerate(OTHERS):
            copies.append(
                send(
                    gram_out.at[turn], gram_in.at[turn, k], ga_s.at[turn, k], ga_r.at[turn, k],
                    (row, column_of(dz, dc)),
                )
            )
            copies[-1].start()
        return copies

    def gram_across(group, turn):
        arrivals(group)
        total = sum((gram_in[turn, k].astype(F32) for k in range(7)), gram_out[turn].astype(F32))
        cross_out[turn] = total.astype(BF16)
        copies = []
        for k, (dy, dx) in enumerate(row_offsets):
            copies.append(
                send(cross_out.at[turn], cross_in.at[turn, k], gb_s.at[turn, k], gb_r.at[turn, k], (chip(dy, dx), col))
            )
            copies[-1].start()
        return copies

    def gram_factor(across, turn):
        arrivals(across)
        total = sum((cross_in[turn, k].astype(F32) for k in range(15)), cross_out[turn].astype(F32))
        return inverse_factor(unpack(total) / sites)

    parts, started = product(first, 0)
    gathers, gram = [], jnp.zeros((64, 64), F32)
    for half in range(2):
        values = summed(parts, 0, half)
        second[row * 2 + half] = (values * own_scale[half]).astype(BF16)
        gathers.append(gather_start(second, 1, half))
        gram += local_gram(values)
    sent = started + deg_copies + scale_copies
    group = gram_to_group(gram, 0)
    gather_forward(second, 1, 0, gathers[0], NEAR_FAR[0])
    gather_forward(second, 1, 0, gathers[0], NEAR_FAR[1])
    gather_forward(second, 1, 1, gathers[1], NEAR_FAR[0])
    gather_forward(second, 1, 0, gathers[0], NEAR_FAR[2])
    gather_forward(second, 1, 1, gathers[1], NEAR_FAR[1])
    gather_forward(second, 1, 1, gathers[1], NEAR_FAR[2])
    for half in range(2):
        gather_end(second, 1, half, gathers[half])
    across = gram_across(group, 0)
    sent += group + across

    parts, started = product(second, 1)
    inverse = gram_factor(across, 0)
    gram = jnp.zeros((64, 64), F32)
    for half in range(2):
        values = jnp.dot(inverse, summed(parts, 1, half), precision=HIGHEST, preferred_element_type=F32)
        grown[half] = values
        gram += local_gram(values)
    sent += started

    group = gram_to_group(gram, 1)
    across = gram_across(group, 1)
    for copy in sent + group:
        copy.wait_send()
    inverse = gram_factor(across, 1)
    for half in range(2):
        out[:, half * 256 : (half + 1) * 256] = jnp.dot(
            inverse, grown[half], precision=HIGHEST, preferred_element_type=F32
        )
    for copy in across:
        copy.wait_send()


def per_device(panel, blocks, columns, counts):
    live = jnp.arange(columns.shape[2], dtype=jnp.int32)[:, None] < jnp.transpose(counts)
    table = jnp.where(live, jnp.transpose(columns[:, 0]), DEAD)
    dma = pltpu.SemaphoreType.DMA
    return pl.pallas_call(
        kernel,
        out_shape=jax.ShapeDtypeStruct(panel.shape, F32),
        in_specs=[pl.BlockSpec(memory_space=pl.ANY)] * 3,
        out_specs=pl.BlockSpec(memory_space=pltpu.VMEM),
        scratch_shapes=[
            pltpu.VMEM((128, 256, 256), BF16),
            pltpu.VMEM((64, 512), F32),
            pltpu.SMEM((8, 16), jnp.int32),
            pltpu.VMEM((33, 64, 256), BF16),
            pltpu.VMEM((33, 64, 256), BF16),
            pltpu.VMEM((32, 1, 256), F32),
            pltpu.VMEM((2, 1, 256), F32),
            pltpu.VMEM((8, 2, 1, 256), F32),
            pltpu.VMEM((7, 2, 1, 256), F32),
            pltpu.VMEM((2, 2, 4, 64, 256), BF16),
            pltpu.VMEM((2, 2, 4, 64, 256), BF16),
            pltpu.VMEM((2, 2, 3, 64, 256), BF16),
            pltpu.VMEM((2, 2, 3, 64, 256), BF16),
            pltpu.VMEM((2, 64, 256), F32),
            pltpu.VMEM((2, 32, 128), BF16),
            pltpu.VMEM((2, 7, 32, 128), BF16),
            pltpu.VMEM((2, 32, 128), BF16),
            pltpu.VMEM((2, 15, 32, 128), BF16),
            pltpu.VMEM((2, 64, 256), F32),
            dma((2,)),
            dma((16,)),
            dma((7,)),
            dma((7,)),
            dma((15,)),
            dma((15,)),
            dma((2, 2, 30)),
            dma((2, 2, 2, 16)),
            dma((2, 2, 2)),
            dma((2, 2, 2)),
            dma((2, 2, 3)),
            dma((2, 2, 3)),
            dma((2, 7)),
            dma((2, 7)),
            dma((2, 15)),
            dma((2, 15)),
        ],
        compiler_params=pltpu.CompilerParams(
            collective_id=0, has_side_effects=True, vmem_limit_bytes=48 * 2**20
        ),
    )(panel, blocks, table)


def solution(mesh):
    in_specs = (
        P(None, ("row", "col")),
        P("row", "col", None, None, None),
        P("row", "col", None),
        P("row", "col"),
    )
    return jax.shard_map(
        per_device, mesh=mesh, in_specs=in_specs, out_specs=P(None, ("row", "col")), check_vma=False
    )
```

```python
import functools

import jax
import jax.numpy as jnp
from jax import lax
from jax.experimental import pallas as pl
from jax.experimental.pallas import tpu as pltpu
from jax.sharding import PartitionSpec as P

MESH = pl.DeviceIdType.MESH
HIGHEST = lax.Precision.HIGHEST
F32 = jnp.float32
BF16 = jnp.bfloat16
NT = (((1,), (1,)), ((), ()))
SIDE = 4
ENTRY = 5
DEAD = 32
PANEL = 16

COL_ORDER = ((2, 0), (2, 1), (1, 0), (1, 1), (3, 0), (3, 1), (0, 1), (0, 0))
OTHERS = COL_ORDER[:-1]
Z_ORDER = (2, 1, 3)
FAR, NEAR = pl.ds(0, 3), pl.ds(3, 1)
NEAR_FAR = (1, 3, 2)
PARTS = (2, 2)


def inverse_factor(gram):
    size = gram.shape[0]
    rows = lax.broadcasted_iota(jnp.int32, (size, size), 0)
    lanes = lax.broadcasted_iota(jnp.int32, (size, size), 1)
    rest = jnp.concatenate([gram, (rows == lanes).astype(F32)], axis=1)
    done = []
    for first in range(0, size, PANEL):
        below = lax.broadcasted_iota(jnp.int32, rest.shape, 0)
        column = [jnp.broadcast_to(rest[:, first + q : first + q + 1], rest.shape) for q in range(PANEL)]
        pivots = []
        for q in range(PANEL):
            pivot = column[q][q : q + 1]
            pivots.append(pivot)
            factor = jnp.where(below > q, column[q] * (1.0 / pivot), 0.0)
            rest = rest - factor * rest[q : q + 1]
            for later in range(q + 1, PANEL):
                column[later] = column[later] - factor * column[later][q : q + 1]
        done.append(rest[:PANEL, size:] * lax.rsqrt(jnp.concatenate(pivots, axis=0)[:, size:]))
        rest = rest[PANEL:]
    return jnp.concatenate(done, axis=0)


def pack(gram):
    half = gram.shape[0] // 2
    return jnp.concatenate([gram[:half], gram[half:]], axis=1)


def unpack(packed):
    width = packed.shape[1] // 2
    return jnp.concatenate([packed[:, :width], packed[:, width:]], axis=0)


def kernel(
    panel, blocks, table_in, out,
    stored, start, table, first, second, scales, own_scale, deg_out, deg_in, pair_out, pair_in, far_out, far_in, part_own,
    gram_out, gram_in, cross_out, cross_in, grown,
    small_sem, load_sem, deg_s, deg_r, scale_s, scale_r, gather_s, gather_r, pair_s, pair_r, far_s, far_r,
    ga_s, ga_r, gb_s, gb_r,
):
    row, col = lax.axis_index("row"), lax.axis_index("col")
    y, x = row // SIDE, row % SIDE
    z, core = col // 2, col % 2
    slots = table.shape[0]
    sites = 65536

    def chip(dy, dx):
        return ((y + dy) % SIDE) * SIDE + (x + dx) % SIDE

    def column_of(dz, dc):
        return ((z + dz) % SIDE) * 2 + (core + dc) % 2

    def send(src, dst, send_sem, recv_sem, to):
        return pltpu.make_async_remote_copy(
            src_ref=src, dst_ref=dst, send_sem=send_sem, recv_sem=recv_sem, device_id=to, device_id_type=MESH
        )

    def arrivals(copies):
        for copy in copies:
            copy.wait_recv()

    small = [
        pltpu.make_async_copy(panel, start, small_sem.at[0]),
        pltpu.make_async_copy(table_in, table, small_sem.at[1]),
    ]
    by_owner = [column_of(dz, dc) * 2 + half for dz, dc in COL_ORDER for half in range(2)]
    loads = [
        pltpu.make_async_copy(blocks.at[i, 0], stored.at[pl.ds(i * slots, slots)], load_sem.at[n])
        for n, i in enumerate(by_owner)
    ]
    for load in small + loads:
        load.start()

    barrier = pltpu.get_barrier_semaphore()
    row_offsets = [(dy, dx) for dy in (2, 1, 3, 0) for dx in (2, 1, 3, 0) if (dy, dx) != (0, 0)]
    for dy, dx in row_offsets:
        pl.semaphore_signal(barrier, inc=1, device_id=(chip(dy, dx), col), device_id_type=MESH)
    for dz, dc in OTHERS:
        pl.semaphore_signal(barrier, inc=1, device_id=(row, column_of(dz, dc)), device_id_type=MESH)

    mine = pl.ds(row * 2, 2)
    first[DEAD] = jnp.zeros_like(first[DEAD])
    second[DEAD] = jnp.zeros_like(second[DEAD])
    for load in small:
        load.wait()
    for half in range(2):
        first[row * 2 + half] = start[:, half * 256 : (half + 1) * 256].astype(BF16)

    def vectors(turn, part):
        size = 64 // PARTS[turn]
        return pl.ds(part * size, size)

    def forward(buf, turn, half, part, src, to, copies):
        (sy, sx), (ty, tx) = src, to
        piece = buf.at[chip(SIDE - sy, SIDE - sx) * 2 + half, vectors(turn, part)]
        arrives = ((sy + ty) % SIDE) * SIDE + (sx + tx) % SIDE
        copies.append(
            send(
                piece, piece, gather_s.at[turn, half, len(copies)], gather_r.at[turn, half, part, arrives],
                (chip(ty, tx), col),
            )
        )
        copies[-1].start()

    def turned(turn, half, part, one, other):
        along_x = half == 0 if PARTS[turn] == 1 else part % 2 == 0
        return (other, one) if along_x else (one, other)

    def gather_start(buf, turn, half):
        copies = []
        for d in NEAR_FAR:
            for part in range(PARTS[turn]):
                forward(buf, turn, half, part, (0, 0), turned(turn, half, part, d, 0), copies)
        for d in NEAR_FAR:
            for part in range(PARTS[turn]):
                forward(buf, turn, half, part, (0, 0), turned(turn, half, part, 0, d), copies)
        return copies

    def arrived(buf, turn, half, part, offset):
        dy, dx = offset
        piece = buf.at[chip(SIDE - dy, SIDE - dx) * 2 + half, vectors(turn, part)]
        send(
            piece, piece, gather_s.at[turn, half, 0], gather_r.at[turn, half, part, dy * SIDE + dx], (row, col)
        ).wait_recv()

    def gather_forward(buf, turn, half, copies, d):
        for part in range(PARTS[turn]):
            arrived(buf, turn, half, part, turned(turn, half, part, d, 0))
            for e in NEAR_FAR:
                forward(buf, turn, half, part, turned(turn, half, part, d, 0), turned(turn, half, part, 0, e), copies)

    def gather_end(buf, turn, half, copies):
        for e in NEAR_FAR:
            for d in range(SIDE):
                for part in range(PARTS[turn]):
                    arrived(buf, turn, half, part, turned(turn, half, part, d, e))
        for copy in copies:
            copy.wait_send()

    gathers, deg_copies, begun = [], [], 0
    for n, i in enumerate(by_owner):
        if n == ENTRY:
            pl.semaphore_wait(barrier, len(row_offsets) + len(OTHERS))
            gathers = [gather_start(first, 0, half) for half in range(2)]
        loads[n].wait()
        total = jnp.zeros((8, 256), F32)
        for s in range(slots):
            alive = jnp.where(table[s, i] < DEAD, 1.0, 0.0).astype(F32)
            block = stored[i * slots + s].T
            stored[i * slots + s] = block
            total += jnp.sum(jnp.abs(block).astype(F32).reshape(32, 8, 256), axis=0) * alive
        deg_out[n // 2, n % 2] = jnp.sum(total, axis=0, keepdims=True)
        if n % 2 == 1 and n // 2 < len(OTHERS):
            k = n // 2
            deg_copies.append(
                send(deg_out.at[k], deg_in.at[k], deg_s.at[k], deg_r.at[k], (row, column_of(*COL_ORDER[k])))
            )
        if n >= ENTRY:
            for copy in deg_copies[begun:]:
                copy.start()
            begun = len(deg_copies)

    for d in NEAR_FAR[:2]:
        for half in range(2):
            gather_forward(first, 0, half, gathers[half], d)
    arrivals(deg_copies)
    degree = sum((deg_in[k] for k in range(7)), deg_out[7])
    own_scale[...] = 1.0 / jnp.sqrt(degree)
    scales[mine] = own_scale[...]
    scale_copies = []
    for k, (dy, dx) in enumerate(row_offsets):
        scale_copies.append(send(own_scale, scales.at[mine], scale_s.at[k], scale_r.at[k], (chip(dy, dx), col)))
        scale_copies[-1].start()
    for d in NEAR_FAR[2:]:
        for half in range(2):
            gather_forward(first, 0, half, gathers[half], d)
    for half in range(2):
        gather_end(first, 0, half, gathers[half])
    for k, (dy, dx) in enumerate(row_offsets):
        theirs = pl.ds(chip(SIDE - dy, SIDE - dx) * 2, 2)
        send(own_scale, scales.at[theirs], scale_s.at[k], scale_r.at[k], (row, col)).wait_recv()

    def scale_block(g, carry):
        first[g] = (first[g].astype(F32) * scales[g]).astype(BF16)
        return carry

    lax.fori_loop(0, 32, scale_block, 0, unroll=4)

    def block_row(buf, i):
        total = jnp.zeros((64, 256), F32)
        for s in range(slots):
            total += jnp.dot(buf[table[s, i]], stored[i * slots + s], preferred_element_type=F32)
        return total

    def row_group(buf, wanted):
        return [block_row(buf, column_of(dz, dc) * 2 + half) for dz, dc, half in wanted]

    def to_other_core(turn, half, which):
        src, dst = pair_out.at[turn, half, which], pair_in.at[turn, half, which]
        k = 0 if which == FAR else 1
        copy = send(src, dst, pair_s.at[turn, half, k], pair_r.at[turn, half, k], (row, column_of(0, 1)))
        copy.start()
        return copy

    def product(buf, turn):
        pairs, fars = [], []
        for half in range(2):
            for k, total in enumerate(row_group(buf, [(dz, 1, half) for dz in Z_ORDER])):
                pair_out[turn, half, k] = total.astype(BF16)
            pairs.append(to_other_core(turn, half, FAR))
            totals = row_group(buf, [(dz, 0, half) for dz in Z_ORDER])
            pairs[half].wait_recv()
            for k, total in enumerate(totals):
                far_out[turn, half, k] = (total + pair_in[turn, half, k].astype(F32)).astype(BF16)
            fars.append([])
            for k, dz in enumerate(Z_ORDER):
                fars[half].append(
                    send(
                        far_out.at[turn, half, k], far_in.at[turn, half, k], far_s.at[turn, half, k],
                        far_r.at[turn, half, k], (row, column_of(dz, 0)),
                    )
                )
                fars[half][-1].start()
        totals = row_group(buf, [(0, 1, 0), (0, 1, 1), (0, 0, 0), (0, 0, 1)])
        for half in range(2):
            pair_out[turn, half, len(Z_ORDER)] = totals[half].astype(BF16)
            part_own[half] = totals[2 + half]
        near = [to_other_core(turn, half, NEAR) for half in range(2)]
        return [[near[half]] + fars[half] for half in range(2)], pairs + near + fars[0] + fars[1]

    def summed(started, turn, half):
        arrivals(started[half])
        total = part_own[half] + pair_in[turn, half, len(Z_ORDER)].astype(F32)
        for k in range(len(Z_ORDER)):
            total += far_in[turn, half, k].astype(F32)
        return total * own_scale[half]

    def local_gram(values):
        return lax.dot_general(values, values, NT, precision=HIGHEST, preferred_element_type=F32)

    def gram_to_group(gram, turn):
        gram_out[turn] = pack(gram).astype(BF16)
        copies = []
        for k, (dz, dc) in enumerate(OTHERS):
            copies.append(
                send(
                    gram_out.at[turn], gram_in.at[turn, k], ga_s.at[turn, k], ga_r.at[turn, k],
                    (row, column_of(dz, dc)),
                )
            )
            copies[-1].start()
        return copies

    def gram_across(group, turn):
        arrivals(group)
        total = sum((gram_in[turn, k].astype(F32) for k in range(7)), gram_out[turn].astype(F32))
        cross_out[turn] = total.astype(BF16)
        copies = []
        for k, (dy, dx) in enumerate(row_offsets):
            copies.append(
                send(cross_out.at[turn], cross_in.at[turn, k], gb_s.at[turn, k], gb_r.at[turn, k], (chip(dy, dx), col))
            )
            copies[-1].start()
        return copies

    def gram_factor(across, turn):
        arrivals(across)
        total = sum((cross_in[turn, k].astype(F32) for k in range(15)), cross_out[turn].astype(F32))
        return inverse_factor(unpack(total) / sites)

    parts, started = product(first, 0)
    gathers, gram = [], jnp.zeros((64, 64), F32)
    for half in range(2):
        values = summed(parts, 0, half)
        second[row * 2 + half] = (values * own_scale[half]).astype(BF16)
        gathers.append(gather_start(second, 1, half))
        gram += local_gram(values)
    sent = started + deg_copies + scale_copies
    group = gram_to_group(gram, 0)
    gather_forward(second, 1, 0, gathers[0], NEAR_FAR[0])
    gather_forward(second, 1, 0, gathers[0], NEAR_FAR[1])
    gather_forward(second, 1, 1, gathers[1], NEAR_FAR[0])
    gather_forward(second, 1, 0, gathers[0], NEAR_FAR[2])
    gather_forward(second, 1, 1, gathers[1], NEAR_FAR[1])
    gather_forward(second, 1, 1, gathers[1], NEAR_FAR[2])
    for half in range(2):
        gather_end(second, 1, half, gathers[half])
    across = gram_across(group, 0)
    sent += group + across

    parts, started = product(second, 1)
    inverse = gram_factor(across, 0)
    gram = jnp.zeros((64, 64), F32)
    for half in range(2):
        values = jnp.dot(inverse, summed(parts, 1, half), precision=HIGHEST, preferred_element_type=F32)
        grown[half] = values
        gram += local_gram(values)
    sent += started

    group = gram_to_group(gram, 1)
    across = gram_across(group, 1)
    for copy in sent + group:
        copy.wait_send()
    inverse = gram_factor(across, 1)
    for half in range(2):
        out[:, half * 256 : (half + 1) * 256] = jnp.dot(
            inverse, grown[half], precision=HIGHEST, preferred_element_type=F32
        )
    for copy in across:
        copy.wait_send()


def per_device(panel, blocks, columns, counts):
    live = jnp.arange(columns.shape[2], dtype=jnp.int32)[:, None] < jnp.transpose(counts)
    table = jnp.where(live, jnp.transpose(columns[:, 0]), DEAD)
    dma = pltpu.SemaphoreType.DMA
    return pl.pallas_call(
        kernel,
        out_shape=jax.ShapeDtypeStruct(panel.shape, F32),
        in_specs=[pl.BlockSpec(memory_space=pl.ANY)] * 3,
        out_specs=pl.BlockSpec(memory_space=pltpu.VMEM),
        scratch_shapes=[
            pltpu.VMEM((128, 256, 256), BF16),
            pltpu.VMEM((64, 512), F32),
            pltpu.SMEM((8, 16), jnp.int32),
            pltpu.VMEM((33, 64, 256), BF16),
            pltpu.VMEM((33, 64, 256), BF16),
            pltpu.VMEM((32, 1, 256), F32),
            pltpu.VMEM((2, 1, 256), F32),
            pltpu.VMEM((8, 2, 1, 256), F32),
            pltpu.VMEM((7, 2, 1, 256), F32),
            pltpu.VMEM((2, 2, 4, 64, 256), BF16),
            pltpu.VMEM((2, 2, 4, 64, 256), BF16),
            pltpu.VMEM((2, 2, 3, 64, 256), BF16),
            pltpu.VMEM((2, 2, 3, 64, 256), BF16),
            pltpu.VMEM((2, 64, 256), F32),
            pltpu.VMEM((2, 32, 128), BF16),
            pltpu.VMEM((2, 7, 32, 128), BF16),
            pltpu.VMEM((2, 32, 128), BF16),
            pltpu.VMEM((2, 15, 32, 128), BF16),
            pltpu.VMEM((2, 64, 256), F32),
            dma((2,)),
            dma((16,)),
            dma((7,)),
            dma((7,)),
            dma((15,)),
            dma((15,)),
            dma((2, 2, 30)),
            dma((2, 2, 2, 16)),
            dma((2, 2, 2)),
            dma((2, 2, 2)),
            dma((2, 2, 3)),
            dma((2, 2, 3)),
            dma((2, 7)),
            dma((2, 7)),
            dma((2, 15)),
            dma((2, 15)),
        ],
        compiler_params=pltpu.CompilerParams(
            collective_id=0, has_side_effects=True, vmem_limit_bytes=48 * 2**20
        ),
    )(panel, blocks, table)


def solution(mesh):
    in_specs = (
        P(None, ("row", "col")),
        P("row", "col", None, None, None),
        P("row", "col", None),
        P("row", "col"),
    )
    return jax.shard_map(
        per_device, mesh=mesh, in_specs=in_specs, out_specs=P(None, ("row", "col")), check_vma=False
    )
```
